512 devices in a mesh: section: 8 (over y), dp: 16 (over z, core), mp: 4 (over x).
Axes of the slice: x: 4, y: 8, z: 8, core: 2. Of those that a mesh axis runs over, the one named last changes fastest.
Arguments:
- activations: bfloat16 [8, 2, 2048, 8192], P('section', None, 'dp', 'mp'), may hold values from -6 to 6
- cotangent: bfloat16 [8, 2, 2048, 1024], P('section', None, 'dp', 'mp'), may hold values from -6 to 6
- base_weight: bfloat16 [8, 8192, 1024], P('section', 'mp', 'dp'), may hold values from -0.0625 to 0.0625
- adapter_down: bfloat16 [8, 32, 8192, 64], P('section', 'dp', 'mp'), may hold values from -0.0625 to 0.0625
- adapter_up: bfloat16 [8, 32, 64, 1024], P('section', 'dp', None, 'mp'), may hold values from -0.75 to 0.75
- slot_language: int32 [8, 32], P('section'), may hold values from 0 to 31, each once within a row
- block_language: int32 [8, 2, 16], P('section', None, 'dp'), may hold values from 0 to 32, as said below
Outputs:
- layer_out: bfloat16 [8, 2, 2048, 1024], P('section', None, 'dp', 'mp')
- input_gradient: bfloat16 [8, 2, 2048, 8192], P('section', None, 'dp', 'mp')
- grad_sum: float32 [8, 32, 64, 1024], P('section', 'dp', None, 'mp')
- grad_square: float32 [8, 32, 64, 1024], P('section', 'dp', None, 'mp')
The draws below stay inside these ranges and needn't reach their ends.
Inputs may be any that keep to these rules, and one draw needn't show every extreme that they name: `block_language`: within each micro-batch of a section the ids never fall along the blocks; padding blocks (32) stand at the end, one or more in every micro-batch, and at least 8 blocks are live.
All inputs are finite; a program needn't handle non-finite values.
Results may differ from the reference program's by a relative error of at most 0.011.
Values may be sent and summed in bfloat16 or wider, within the bound.
No kernel may reach another device: no remote copies, remote signals or barrier semaphores. Data moves between devices by JAX's collectives and lax.ppermute only.
A program may use at most 64 MiB of HBM per device.

```python
import jax
import jax.numpy as jnp
from jax import lax

MODEL_WIDTH = 8192
KVW = 1024
R = 64
LANG = 32
BLOCK_ROWS = 128
MICRO_BATCHES = 2
SECTIONS = 8
TOKEN_ROWS = 2048
NB_DEV = 1
NBLK = 16


def draw_block_language(key, part):
    key = jax.random.fold_in(key, 7)
    key_one, key_two, key_three, key_perm, key_live = jax.random.split(key, 5)
    shape = (SECTIONS, MICRO_BATCHES, NBLK)
    first = jax.random.randint(key_one, shape, 0, LANG)
    second = jax.random.randint(key_two, shape, 0, LANG)
    third = jax.random.randint(key_three, shape, 0, LANG)
    lowest = jnp.minimum(jnp.minimum(first, second), third)
    order = jax.random.permutation(key_perm, LANG).astype(jnp.int32)
    picked = order[lowest]
    ranked = jnp.sort(picked, axis=-1)
    live_count = jax.random.randint(key_live, (SECTIONS, MICRO_BATCHES, 1), NBLK // 2, NBLK)
    positions = jnp.arange(NBLK, dtype=jnp.int32)[None, None, :]
    return jnp.where(positions < live_count, ranked, LANG).astype(jnp.int32)


def shard_levels(key, extent, cuts, low, high):
    gain = 1.0
    for position, shards_of in cuts:
        draws = jax.random.uniform(jax.random.fold_in(jax.random.fold_in(key, 6), position), (shards_of,), jnp.float32, low / len(cuts), high / len(cuts))
        gain = gain * jnp.repeat(jnp.exp(draws), extent[position] // shards_of).reshape((-1,) + (1,) * (len(extent) - 1 - position))
    return gain


def bell_draw(rng, shape, scale, bound, pieces=(), held_as=jnp.bfloat16):
    level = shard_levels(rng, shape, pieces, -0.22, 0.18) if pieces else 1.0
    entries = jax.random.normal(rng, shape, jnp.float32) * scale * level
    return jnp.minimum(jnp.maximum(entries, -bound), bound).astype(held_as)


def setup_inputs(seed: int = 0) -> dict:
    key_of = jax.random.split(jax.random.key(seed), 8)
    activations = bell_draw(key_of[0], (SECTIONS, MICRO_BATCHES, TOKEN_ROWS, MODEL_WIDTH), 1.0, 6.0, ((0, 8), (2, 16), (3, 4)))
    cotangent = bell_draw(key_of[1], (SECTIONS, MICRO_BATCHES, TOKEN_ROWS, KVW), 1.0, 6.0, ((0, 8), (2, 16), (3, 4)))
    base_weight = bell_draw(key_of[2], (SECTIONS, MODEL_WIDTH, KVW), MODEL_WIDTH ** -0.5, 0.0625, ((0, 8), (1, 4), (2, 16)))
    adapter_down = bell_draw(key_of[3], (SECTIONS, LANG, MODEL_WIDTH, R), MODEL_WIDTH ** -0.5, 0.0625, ((0, 8), (1, 16), (2, 4)))
    adapter_up = bell_draw(key_of[4], (SECTIONS, LANG, R, KVW), R ** -0.5, 0.75, ((0, 8), (1, 16), (3, 4)))
    slot_language = jax.vmap(lambda own: jax.random.permutation(own, LANG))(jax.random.split(key_of[5], SECTIONS)).reshape((SECTIONS, LANG)).astype(jnp.int32)
    block_language = draw_block_language(jax.random.fold_in(key_of[7], 71), 0)
    return dict(activations=activations, cotangent=cotangent, base_weight=base_weight, adapter_down=adapter_down, adapter_up=adapter_up, slot_language=slot_language, block_language=block_language)


adapter_scale = 2.0


def one_section(inputs):
    acts, cots, weight, downs, ups, slot_table, langs = inputs
    block_total = MICRO_BATCHES * NBLK
    block_langs = langs.reshape(block_total)
    lane_ids = jnp.arange(LANG, dtype=jnp.int32)
    slot_match = slot_table[None, :] == block_langs[:, None]
    live_blocks = block_langs < LANG
    slot_index = jnp.sum(jnp.where(slot_match, lane_ids[None, :], 0), axis=1).astype(jnp.int32)
    block_down_weight = downs[slot_index].astype(jnp.float32)
    block_up_weight = ups[slot_index].astype(jnp.float32)
    flat_acts = acts.reshape(MICRO_BATCHES * TOKEN_ROWS, MODEL_WIDTH)
    flat_cots = cots.reshape(MICRO_BATCHES * TOKEN_ROWS, KVW)
    frozen_output = jnp.dot(flat_acts, weight, preferred_element_type=jnp.float32).reshape(block_total, BLOCK_ROWS, KVW)
    frozen_backward = jnp.dot(flat_cots, weight.T, preferred_element_type=jnp.float32).reshape(block_total, BLOCK_ROWS, MODEL_WIDTH)
    acts_wide = flat_acts.reshape(block_total, BLOCK_ROWS, MODEL_WIDTH).astype(jnp.float32)
    wide_cotangents = flat_cots.reshape(block_total, BLOCK_ROWS, KVW).astype(jnp.float32)
    upper_limit = lax.Precision.HIGHEST
    down_rank = jnp.einsum('nbd,ndr->nbr', acts_wide, block_down_weight, precision=upper_limit)
    up_rank = jnp.einsum('nbk,nrk->nbr', wide_cotangents, block_up_weight, precision=upper_limit)
    down_rank_weight = lax.optimization_barrier(down_rank.astype(jnp.bfloat16)).astype(jnp.float32)
    up_rank_weight = lax.optimization_barrier(up_rank.astype(jnp.bfloat16)).astype(jnp.float32)
    retain_mask = live_blocks[:, None, None]
    forward_pass = frozen_output + adapter_scale * jnp.einsum('pqe,pec->pqc', down_rank_weight, block_up_weight, precision=upper_limit)
    layer_out = jnp.where(retain_mask, forward_pass, 0.0).astype(jnp.bfloat16).reshape(MICRO_BATCHES, TOKEN_ROWS, KVW)
    adapter_backward = adapter_scale * jnp.einsum('tks,tjs->tkj', up_rank_weight, block_down_weight, precision=upper_limit)
    adapter_backward = lax.optimization_barrier(adapter_backward.astype(jnp.bfloat16)).astype(jnp.float32)
    input_gradient = jnp.where(retain_mask, frozen_backward + adapter_backward, 0.0).astype(jnp.bfloat16).reshape(MICRO_BATCHES, TOKEN_ROWS, MODEL_WIDTH)
    block_gradient = (adapter_scale / BLOCK_ROWS) * jnp.einsum('sdi,sdj->sij', down_rank_weight, wide_cotangents, precision=upper_limit)
    holders = NBLK // NB_DEV
    onehot = slot_match.astype(jnp.float32).reshape(MICRO_BATCHES, holders, NB_DEV, LANG)
    device_grads = jnp.einsum('mdnl,mdnrk->dlrk', onehot, block_gradient.reshape(MICRO_BATCHES, holders, NB_DEV, R, KVW), precision=upper_limit)
    return layer_out, input_gradient, jnp.sum(device_grads, axis=0), jnp.sum(device_grads * device_grads, axis=0)


def reference(activations, cotangent, base_weight, adapter_down, adapter_up, slot_language, block_language):
    inputs = jnp.roll(activations, 1, axis=0)
    incoming = jnp.roll(cotangent, -1, axis=0)
    layer_out, input_gradient, grad_sum, grad_square = lax.map(one_section, (inputs, incoming, base_weight, adapter_down, adapter_up, slot_language, block_language))
    return (layer_out, input_gradient, grad_sum, grad_square)
```

```python
import jax
import jax.numpy as jnp
from jax import lax
from jax.sharding import PartitionSpec as P

BLOCK_ROWS = 128
LANES = 128

adapter_scale = 2.0


def passed_along(array, axis, by):
    devices = lax.axis_size(axis)
    return lax.ppermute(array, axis, [(i, (i + by) % devices) for i in range(devices)])


def shards(
    activations, cotangent, base_weight, adapter_down, adapter_up, slot_language, block_language
):
    bf16, f32 = jnp.bfloat16, jnp.float32
    holders = lax.axis_size("dp")
    quarters = lax.axis_size("mp")
    own_slots, width, rank = adapter_down.shape[1:]
    columns = adapter_up.shape[3]
    micro = activations.shape[1]
    rows = micro * BLOCK_ROWS
    piece = width // holders
    up_groups = holders // (columns // LANES)
    up_rows = rank // up_groups
    me = lax.axis_index("dp")

    arrived = passed_along(activations, "section", 1)[0]
    returned = passed_along(cotangent, "section", -1)[0]

    slot_table = slot_language[0]
    langs = block_language[0, :, 0]
    live = langs < slot_table.shape[0]

    down_pieces = (
        jnp.swapaxes(adapter_down[0], 1, 2)
        .reshape(own_slots, rank, holders, piece)
        .transpose(2, 0, 1, 3)
        .reshape(holders, own_slots * rank, piece)
    )
    up_pieces = (
        adapter_up[0]
        .reshape(own_slots, up_groups, up_rows, columns // LANES, LANES)
        .transpose(1, 3, 0, 2, 4)
        .reshape(holders, own_slots * up_rows, LANES)
    )
    lang_rows = jnp.broadcast_to(
        langs.astype(bf16)[None, :, None], (holders, micro, LANES)
    )
    lang_rows = jnp.pad(lang_rows, ((0, 0), (0, 16 - micro), (0, 0)))
    first = jnp.concatenate([down_pieces, up_pieces, lang_rows], axis=1)
    first = lax.all_to_all(first, "dp", split_axis=0, concat_axis=0, tiled=True)

    down_end = own_slots * rank
    up_end = down_end + own_slots * up_rows
    all_langs = first[:, up_end : up_end + micro, 0].astype(jnp.int32)
    match = all_langs.reshape(-1)[:, None] == slot_table[None, :]
    slots = jnp.sum(
        jnp.where(match, jnp.arange(slot_table.shape[0], dtype=jnp.int32)[None, :], 0), axis=1
    )
    held_down = first[:, :down_end].reshape(holders * own_slots, rank, piece)
    held_up = first[:, down_end:up_end].reshape(holders * own_slots, up_rows, LANES)
    second = jnp.concatenate(
        [
            held_down[slots].reshape(holders, micro * rank, piece),
            held_up[slots].reshape(holders, micro * up_rows, LANES),
        ],
        axis=1,
    )
    second = lax.all_to_all(second, "dp", split_axis=0, concat_axis=0, tiled=True)
    down = (
        second[:, : micro * rank]
        .reshape(holders, micro, rank, piece)
        .transpose(1, 2, 0, 3)
        .reshape(micro, rank, width)
    )
    up = (
        second[:, micro * rank :]
        .reshape(up_groups, columns // LANES, micro, up_rows, LANES)
        .transpose(2, 0, 3, 1, 4)
        .reshape(micro, rank, columns)
    )

    whole_weight = lax.all_gather(base_weight[0], "dp", axis=1, tiled=True)
    all_cots = lax.all_gather(returned, "mp", axis=2, tiled=True)
    flat_acts = arrived.reshape(rows, width)
    base_part = jnp.dot(flat_acts, whole_weight, preferred_element_type=f32).astype(bf16)
    base_part = base_part.reshape(rows, quarters, columns).transpose(1, 0, 2)
    base_parts = lax.all_to_all(base_part, "mp", split_axis=0, concat_axis=0, tiled=True)
    base = jnp.sum(base_parts.astype(f32), axis=0).reshape(micro, BLOCK_ROWS, columns)
    back_base = lax.dot_general(
        all_cots.reshape(rows, whole_weight.shape[1]),
        whole_weight,
        (((1,), (1,)), ((), ())),
        preferred_element_type=f32,
    ).reshape(micro, BLOCK_ROWS, width)

    down_part = jnp.einsum("nrd,nbd->nrb", down, arrived, preferred_element_type=f32)
    up_part = jnp.einsum("nrk,nbk->nrb", up, returned, preferred_element_type=f32)
    parts = jnp.stack([down_part, up_part]).astype(bf16)
    parts = lax.all_gather(parts, "mp", axis=0, tiled=False)
    ranks = jnp.sum(parts.astype(f32), axis=0).astype(bf16)
    rank_in, rank_back = ranks[0], ranks[1]

    keep = live[:, None, None]
    forward = base + adapter_scale * jnp.einsum(
        "nrb,nrc->nbc", rank_in, up, preferred_element_type=f32
    )
    layer_out = jnp.where(keep, forward, 0.0).astype(bf16)[None]
    lora_back = adapter_scale * jnp.einsum(
        "nrb,nrd->nbd", rank_back, down, preferred_element_type=f32
    )
    input_gradient = jnp.where(keep, back_base + lora_back, 0.0).astype(bf16)[None]

    block_gradient = (
        adapter_scale
        / BLOCK_ROWS
        * jnp.einsum("nrb,nbc->nrc", rank_in, returned, preferred_element_type=f32)
    ).astype(bf16)
    gathered = lax.all_gather(block_gradient, "dp", axis=0, tiled=False).astype(f32)
    own = lax.dynamic_slice_in_dim(slot_table, me * own_slots, own_slots)
    sums, squares = [], []
    for k in range(own_slots):
        hit = (all_langs == own[k])[:, :, None, None]
        partial = jnp.sum(jnp.where(hit, gathered, 0.0), axis=1)
        sums.append(jnp.sum(partial, axis=0))
        squares.append(jnp.sum(partial * partial, axis=0))
    return (layer_out, input_gradient, jnp.stack(sums)[None], jnp.stack(squares)[None])


def solution(mesh):
    in_specs = (
        P("section", None, "dp", "mp"),
        P("section", None, "dp", "mp"),
        P("section", "mp", "dp"),
        P("section", "dp", "mp", None),
        P("section", "dp", None, "mp"),
        P("section", None),
        P("section", None, "dp"),
    )
    out_specs = (
        P("section", None, "dp", "mp"),
        P("section", None, "dp", "mp"),
        P("section", "dp", None, "mp"),
        P("section", "dp", None, "mp"),
    )
    return jax.shard_map(shards, mesh=mesh, in_specs=in_specs, out_specs=out_specs, check_vma=False)
```

```python
import functools

import jax
import jax.numpy as jnp
from jax import lax
from jax.experimental import pallas as pl
from jax.experimental.pallas import tpu as pltpu
from jax.sharding import PartitionSpec as P

BLOCK_ROWS = 128
LANES = 128

adapter_scale = 2.0

bf16, f32 = jnp.bfloat16, jnp.float32
VMEM_LIMIT = 24 * 1024 * 1024
WIDE_LIMIT = 60 * 1024 * 1024


def passed_along(array, axis, by):
    devices = lax.axis_size(axis)
    return lax.ppermute(array, axis, [(i, (i + by) % devices) for i in range(devices)])


def exchanged(array, axis):
    return lax.all_to_all(array, axis, split_axis=0, concat_axis=0, tiled=True)


def smem():
    return pl.BlockSpec(memory_space=pltpu.SMEM)


def params():
    return pltpu.CompilerParams(vmem_limit_bytes=VMEM_LIMIT)


def nt_dot(a, b):
    return lax.dot_general(a, b, (((1,), (1,)), ((), ())), preferred_element_type=f32)


def tn_dot(a, b):
    return lax.dot_general(a, b, (((0,), (0,)), ((), ())), preferred_element_type=f32)


def pack_kernel(halves, langs_ref, table_ref, down_ref, up_ref, out_ref):
    holders, payload, piece = out_ref.shape
    own_slots, rank, _ = down_ref.shape
    micro, count = langs_ref.shape[0], table_ref.shape[1]
    group = rank * halves // holders
    low, high = own_slots * rank, own_slots * (rank + group)
    match = table_ref[...] == langs_ref[...]
    lane = lax.broadcasted_iota(jnp.int32, (micro, count), 1)
    slots = jnp.min(jnp.where(match, lane, count), axis=1, keepdims=True).astype(f32)
    row = lax.broadcasted_iota(jnp.int32, (payload - high, piece), 0)
    marks = jnp.zeros((payload - high, piece), f32)
    for m in range(micro):
        marks = jnp.where(row == m, slots[m : m + 1], marks)
    marks = marks.astype(bf16)
    ups = [up_ref[k].astype(f32) for k in range(own_slots)]
    for p in range(holders):
        for k in range(own_slots):
            out_ref[p, k * rank : (k + 1) * rank, :] = down_ref[k, :, p * piece : (p + 1) * piece]
        top, left = (p // halves) * group, (p % halves) * LANES
        out_ref[p, low:high, :] = jnp.concatenate(
            [up[top : top + group, left : left + LANES] for up in ups], axis=0
        ).astype(bf16)
        out_ref[p, high:, :] = marks


def packed(langs, table, down, up, holders):
    own_slots, rank, width = down.shape
    halves = up.shape[2] // LANES
    payload = own_slots * (rank + rank * halves // holders) + 8
    out = (holders, payload, width // holders)
    return pl.pallas_call(
        functools.partial(pack_kernel, halves),
        grid=(1,),
        out_shape=jax.ShapeDtypeStruct(out, bf16),
        in_specs=[
            pl.BlockSpec(langs.shape, lambda i: (0, 0)),
            pl.BlockSpec(table.shape, lambda i: (0, 0)),
            pl.BlockSpec(down.shape, lambda i: (0, 0, 0)),
            pl.BlockSpec(up.shape, lambda i: (0, 0, 0)),
        ],
        out_specs=pl.BlockSpec(out, lambda i: (0, 0, 0)),
        compiler_params=pltpu.CompilerParams(vmem_limit_bytes=WIDE_LIMIT),
        name="packed_adapters",
    )(langs, table, down, up)


def base_kernel(micro, first_ref, *refs):
    acts, gathered_ref, outs = refs[:micro], refs[micro], refs[micro + 1 :]
    weight = gathered_ref[...].reshape(-1, gathered_ref.shape[2])
    for k, out_ref in enumerate(outs):

        @pl.when(pl.program_id(0) == k)
        def _():
            for m in range(micro):
                out_ref[m] = nt_dot(acts[m][0, 0], weight).astype(bf16)


def base_products(first, acts, gathered, quarters):
    micro = len(acts)
    width = gathered.shape[2]
    holders, cols = gathered.shape[:2]
    group = holders // quarters
    out = (micro, BLOCK_ROWS, group * cols)
    return pl.pallas_call(
        functools.partial(base_kernel, micro),
        grid_spec=pltpu.PrefetchScalarGridSpec(
            num_scalar_prefetch=1,
            grid=(quarters,),
            in_specs=[pl.BlockSpec(acts[0].shape, lambda i, first_ref: (0, 0, 0, 0))] * micro
            + [
                pl.BlockSpec(
                    (group, cols, width),
                    lambda i, first_ref: (lax.rem(first_ref[0] + i, quarters), 0, 0),
                ),
            ],
            out_specs=(pl.BlockSpec(out, lambda i, first_ref: (0, 0, 0)),) * quarters,
        ),
        out_shape=(jax.ShapeDtypeStruct(out, bf16),) * quarters,
        compiler_params=params(),
        cost_estimate=pl.CostEstimate(
            flops=2 * micro * BLOCK_ROWS * width * cols * holders,
            bytes_accessed=2 * holders * cols * (width + 2 * micro * BLOCK_ROWS),
            transcendentals=0,
        ),
        name="base_products",
    )(first, *acts, gathered)


def part_kernel(micro, second_ref, returned_ref, *refs):
    acts, parts_ref, up_ref = refs[:micro], refs[micro], refs[micro + 1]
    pieces, _, piece = second_ref.shape
    rank, columns = up_ref.shape[1:]
    halves = columns // LANES
    group = rank * halves // pieces
    for p in range(pieces):
        both = second_ref[p, micro * rank :, :].astype(f32)
        top, left = (p // halves) * group, (p % halves) * LANES
        for m in range(micro):
            up_ref[m, top : top + group, left : left + LANES] = both[m * group : (m + 1) * group]
    for m in range(micro):
        down = jnp.concatenate(
            [second_ref[p, m * rank : (m + 1) * rank, :] for p in range(pieces)], axis=1
        )
        parts = (
            nt_dot(down, acts[m][0, 0]).astype(bf16),
            nt_dot(up_ref[m].astype(bf16), returned_ref[m]).astype(bf16),
        )
        for q in range(parts_ref.shape[0]):
            for kind in range(2):
                parts_ref[q, kind, m] = parts[kind]


def rank_parts(second, returned, acts, rank, quarters):
    micro, _, columns = returned.shape
    return pl.pallas_call(
        functools.partial(part_kernel, micro),
        out_shape=(
            jax.ShapeDtypeStruct((quarters, 2, micro, rank, BLOCK_ROWS), bf16),
            jax.ShapeDtypeStruct((micro, rank, columns), f32),
        ),
        in_specs=[pl.BlockSpec(memory_space=pltpu.VMEM)] * (2 + micro),
        out_specs=(pl.BlockSpec(memory_space=pltpu.VMEM),) * 2,
        compiler_params=params(),
        name="rank_parts",
    )(second, returned, *acts)


def select_kernel(micro, own_slots, rank, slots_ref, first_ref, out_ref):
    holders = out_ref.shape[0]
    group = out_ref.shape[1] // micro - rank
    low = own_slots * rank
    for d in range(holders):
        ups = []
        for m in range(micro):
            slot = jnp.minimum(slots_ref[d * micro + m], holders * own_slots - 1)
            owner, k = slot // own_slots, slot % own_slots
            rows = pl.ds(pl.multiple_of(k * rank, rank), rank)
            out_ref[d, m * rank : (m + 1) * rank, :] = first_ref[owner, rows, :]
            held = first_ref[owner, low : low + own_slots * group, :].astype(f32)
            up = held[:group]
            for j in range(1, own_slots):
                up = jnp.where(k == j, held[j * group : (j + 1) * group], up)
            ups.append(up)
        out_ref[d, micro * rank :, :] = jnp.concatenate(ups, axis=0).astype(bf16)


def selected(slots, first, micro, own_slots, rank, group):
    holders, _, lanes = first.shape
    return pl.pallas_call(
        functools.partial(select_kernel, micro, own_slots, rank),
        out_shape=jax.ShapeDtypeStruct((holders, micro * (rank + group), lanes), bf16),
        in_specs=[smem(), pl.BlockSpec(memory_space=pltpu.VMEM)],
        out_specs=pl.BlockSpec(memory_space=pltpu.VMEM),
        compiler_params=params(),
        name="selected_pieces",
    )(slots, first)


def gradient_kernel(micro, live_ref, cots_ref, ranks_ref, down_ref, gathered_ref, out_ref):
    rank = ranks_ref.shape[1]
    pieces = down_ref.shape[0]
    cots = jnp.concatenate([cots_ref[q] for q in range(cots_ref.shape[0])], axis=1)
    weight = gathered_ref[...].reshape(-1, gathered_ref.shape[2])
    total = jnp.dot(cots, weight, preferred_element_type=f32)
    for m in range(micro):
        back = (adapter_scale * ranks_ref[m].astype(f32)).T.astype(bf16)
        down = jnp.concatenate(
            [down_ref[p, m * rank : (m + 1) * rank, :] for p in range(pieces)], axis=1
        )
        lora = jnp.dot(back, down, preferred_element_type=f32).astype(bf16).astype(f32)
        part = total[m * BLOCK_ROWS : (m + 1) * BLOCK_ROWS] + lora
        out_ref[m] = jnp.where(live_ref[m] > 0, part, 0.0).astype(bf16)


def input_gradients(live, cots, ranks, second, gathered):
    micro, rank = ranks.shape[:2]
    holders, cols, width = gathered.shape
    pieces, _, piece = second.shape
    steps = 4
    return pl.pallas_call(
        functools.partial(gradient_kernel, micro),
        grid=(steps,),
        out_shape=jax.ShapeDtypeStruct((micro, BLOCK_ROWS, width), bf16),
        in_specs=[
            smem(),
            pl.BlockSpec(cots.shape, lambda i: (0, 0, 0)),
            pl.BlockSpec(ranks.shape, lambda i: (0, 0, 0)),
            pl.BlockSpec((pieces // steps, micro * rank, piece), lambda i: (i, 0, 0)),
            pl.BlockSpec((holders, cols, width // steps), lambda i: (0, 0, i)),
        ],
        out_specs=pl.BlockSpec((micro, BLOCK_ROWS, width // steps), lambda i: (0, 0, i)),
        compiler_params=params(),
        cost_estimate=pl.CostEstimate(
            flops=2 * micro * BLOCK_ROWS * width * cols * holders,
            bytes_accessed=2 * (2 * micro * BLOCK_ROWS * width + holders * cols * width),
            transcendentals=0,
        ),
        name="input_gradients",
    )(live, cots, ranks, second, gathered)


def layer_kernel(micro, live_ref, ranks_ref, up_ref, *refs):
    out_ref = refs[-1]
    for m in range(micro):
        total = adapter_scale * tn_dot(ranks_ref[m], up_ref[m].astype(bf16))
        for part_ref in refs[:-1]:
            total += part_ref[m].astype(f32)
        out_ref[m] = jnp.where(live_ref[m] > 0, total, 0.0).astype(bf16)


def layer_outputs(live, ranks, up, parts):
    micro, _, columns = up.shape
    return pl.pallas_call(
        functools.partial(layer_kernel, micro),
        out_shape=jax.ShapeDtypeStruct((micro, BLOCK_ROWS, columns), bf16),
        in_specs=[smem()] + [pl.BlockSpec(memory_space=pltpu.VMEM)] * (2 + len(parts)),
        out_specs=pl.BlockSpec(memory_space=pltpu.VMEM),
        compiler_params=params(),
        name="layer_outputs",
    )(live, ranks, up, *parts)


def rank_kernel(halves, parts_ref, incoming_ref, ranks_ref, pieces_ref):
    micro, rank = parts_ref.shape[2:4]
    total = parts_ref[0].astype(f32)
    for q in range(1, parts_ref.shape[0]):
        total += parts_ref[q].astype(f32)
    ranks_ref[...] = total.astype(bf16)
    grads = [
        jnp.dot(ranks_ref[0, m], incoming_ref[m], preferred_element_type=f32)
        * (adapter_scale / BLOCK_ROWS)
        for m in range(micro)
    ]
    holders = pieces_ref.shape[0]
    group = rank * halves // holders
    for p in range(holders):
        top, left = (p // halves) * group, (p % halves) * LANES
        pieces_ref[p] = jnp.concatenate(
            [g[top : top + group, left : left + LANES] for g in grads], axis=0
        ).astype(bf16)


def ranks_and_pieces(parts, incoming, holders):
    micro, rank = parts.shape[2:4]
    columns = incoming.shape[2]
    halves = columns // LANES
    group = rank * halves // holders
    return pl.pallas_call(
        functools.partial(rank_kernel, halves),
        out_shape=(
            jax.ShapeDtypeStruct(parts.shape[1:], bf16),
            jax.ShapeDtypeStruct((holders, micro * group, LANES), bf16),
        ),
        in_specs=[pl.BlockSpec(memory_space=pltpu.VMEM)] * 2,
        out_specs=(pl.BlockSpec(memory_space=pltpu.VMEM),) * 2,
        compiler_params=params(),
        name="ranks_and_pieces",
    )(parts, incoming)


def slot_kernel(micro, slots_ref, pieces_ref, out_ref):
    count = out_ref.shape[0]
    holders = pieces_ref.shape[0]
    group = pieces_ref.shape[1] // micro
    out_ref[...] = jnp.zeros_like(out_ref)
    for d in range(holders):
        both = pieces_ref[d].astype(f32)
        marks = [slots_ref[d * micro + m] for m in range(micro)]
        terms = [
            jnp.where(marks[m] < count, both[m * group : (m + 1) * group], 0.0)
            for m in range(micro)
        ]
        slots = [jnp.minimum(mark, count - 1) for mark in marks]
        for m in range(1, micro):
            for n in range(m):
                same = marks[m] == marks[n]
                terms[n] = terms[n] + jnp.where(same, terms[m], 0.0)
                terms[m] = jnp.where(same, 0.0, terms[m])
        for m in range(micro):
            out_ref[slots[m], 0] += terms[m]
            out_ref[slots[m], 1] += terms[m] * terms[m]


def slot_sums(slots, pieces, slot_count, micro):
    group = pieces.shape[1] // micro
    return pl.pallas_call(
        functools.partial(slot_kernel, micro),
        out_shape=jax.ShapeDtypeStruct((slot_count, 2, group, LANES), f32),
        in_specs=[smem(), pl.BlockSpec(memory_space=pltpu.VMEM)],
        out_specs=pl.BlockSpec(memory_space=pltpu.VMEM),
        compiler_params=params(),
        name="slot_sums",
    )(slots, pieces)


def place_kernel(halves, pieces_ref, sum_ref, square_ref):
    holders, own_slots, _, group = pieces_ref.shape[:4]
    for p in range(holders):
        top, left = (p // halves) * group, (p % halves) * LANES
        for k in range(own_slots):
            sum_ref[k, top : top + group, left : left + LANES] = pieces_ref[p, k, 0]
            square_ref[k, top : top + group, left : left + LANES] = pieces_ref[p, k, 1]


def placed(pieces, rank, columns):
    own_slots = pieces.shape[1]
    shape = jax.ShapeDtypeStruct((own_slots, rank, columns), f32)
    return pl.pallas_call(
        functools.partial(place_kernel, columns // LANES),
        out_shape=(shape, shape),
        in_specs=[pl.BlockSpec(memory_space=pltpu.VMEM)],
        out_specs=(pl.BlockSpec(memory_space=pltpu.VMEM),) * 2,
        compiler_params=params(),
        name="placed_sums",
    )(pieces)


def shards(
    activations, cotangent, base_weight, adapter_down, adapter_up, slot_language, block_language
):
    holders = lax.axis_size("dp")
    quarters = lax.axis_size("mp")
    own_slots, width, rank = adapter_down.shape[1:]
    columns = adapter_up.shape[3]
    micro = activations.shape[1]
    rows = micro * BLOCK_ROWS
    piece = width // holders
    up_groups = holders // (columns // LANES)
    up_rows = rank // up_groups
    me = lax.axis_index("dp")

    returned = passed_along(cotangent, "section", -1)[0]
    arrived = [passed_along(activations[:, m : m + 1], "section", 1) for m in range(micro)]

    slot_table = slot_language[0]
    langs = block_language[0, :, 0]
    live = (langs < slot_table.shape[0]).astype(jnp.int32)

    weight = jnp.swapaxes(base_weight[0], 0, 1)
    gathered = lax.all_gather(weight, "dp", axis=0)
    all_cots = lax.all_gather(returned.reshape(rows, columns), "mp", axis=0)

    first = packed(block_language[0], slot_language, jnp.swapaxes(adapter_down[0], 1, 2), adapter_up[0], holders)
    first = exchanged(first, "dp")

    marked = own_slots * (rank + up_rows)
    slots = first[:, marked : marked + micro, 0].astype(jnp.int32).reshape(-1)
    second = selected(slots, first, micro, own_slots, rank, up_rows)
    second, arrived[0] = lax.optimization_barrier((second, arrived[0]))
    second = exchanged(second, "dp")
    second, all_cots = lax.optimization_barrier((second, all_cots))

    parts, up = rank_parts(second, returned, arrived, rank, quarters)
    parts = exchanged(parts, "mp")
    quarter = lax.axis_index("mp").astype(jnp.int32).reshape(1)
    base_parts = base_products(quarter, arrived, gathered, quarters)
    parts, base_parts = lax.optimization_barrier((parts, base_parts))
    ranks, pieces = ranks_and_pieces(parts, returned, holders)
    rank_in, rank_back = ranks[0], ranks[1]

    pieces = exchanged(pieces, "dp")
    input_gradient = input_gradients(live, all_cots, rank_back, second, gathered)[None]
    pieces, input_gradient = lax.optimization_barrier((pieces, input_gradient))
    sums = slot_sums(slots, pieces, slot_table.shape[0], micro)
    sums, base_parts = lax.optimization_barrier((sums, base_parts))
    sums = exchanged(sums, "dp").reshape((holders, own_slots) + sums.shape[1:])
    base_parts = [base_parts[0]] + [
        lax.ppermute(base_parts[k], "mp", [(i, (i + k) % quarters) for i in range(quarters)])
        for k in range(1, quarters)
    ]
    layer_out = layer_outputs(live, rank_in, up, base_parts)[None]
    sums, layer_out = lax.optimization_barrier((sums, layer_out))
    grad_sum, grad_square = placed(sums, rank, columns)

    return (layer_out, input_gradient, grad_sum[None], grad_square[None])


def solution(mesh):
    in_specs = (
        P("section", None, "dp", "mp"),
        P("section", None, "dp", "mp"),
        P("section", "mp", "dp"),
        P("section", "dp", "mp", None),
        P("section", "dp", None, "mp"),
        P("section", None),
        P("section", None, "dp"),
    )
    out_specs = (
        P("section", None, "dp", "mp"),
        P("section", None, "dp", "mp"),
        P("section", "dp", None, "mp"),
        P("section", "dp", None, "mp"),
    )
    return jax.shard_map(shards, mesh=mesh, in_specs=in_specs, out_specs=out_specs, check_vma=False)
```

```python
import functools

import jax
import jax.numpy as jnp
from jax import lax
from jax.experimental import pallas as pl
from jax.experimental.pallas import tpu as pltpu
from jax.sharding import PartitionSpec as P

BLOCK_ROWS = 128
LANES = 128

adapter_scale = 2.0

bf16, f32 = jnp.bfloat16, jnp.float32
VMEM_LIMIT = 24 * 1024 * 1024
WIDE_LIMIT = 60 * 1024 * 1024


def passed_along(array, axis, by):
    devices = lax.axis_size(axis)
    return lax.ppermute(array, axis, [(i, (i + by) % devices) for i in range(devices)])


def exchanged(array, axis):
    return lax.all_to_all(array, axis, split_axis=0, concat_axis=0, tiled=True)


def smem():
    return pl.BlockSpec(memory_space=pltpu.SMEM)


def params():
    return pltpu.CompilerParams(vmem_limit_bytes=VMEM_LIMIT)


def nt_dot(a, b):
    return lax.dot_general(a, b, (((1,), (1,)), ((), ())), preferred_element_type=f32)


def tn_dot(a, b):
    return lax.dot_general(a, b, (((0,), (0,)), ((), ())), preferred_element_type=f32)


def pack_kernel(halves, langs_ref, table_ref, down_ref, up_ref, out_ref):
    pieces, payload, piece = out_ref.shape
    own_slots, rank, _ = down_ref.shape
    micro, count = langs_ref.shape[1], table_ref.shape[1]
    group = up_ref.shape[1] * halves // pieces
    low, high = own_slots * rank, own_slots * (rank + group)
    lane = lax.broadcasted_iota(jnp.int32, (1, count), 1)
    row = lax.broadcasted_iota(jnp.int32, (payload - high, piece), 0)
    marks = jnp.zeros((payload - high, piece), f32)
    for m in range(micro):
        match = table_ref[...] == langs_ref[:, m : m + 1]
        slot = jnp.min(jnp.where(match, lane, count), axis=1, keepdims=True).astype(f32)
        marks = jnp.where(row == m, slot, marks)
    marks = marks.astype(bf16)
    ups = [up_ref[k].astype(f32) for k in range(own_slots)]
    for p in range(pieces):
        for k in range(own_slots):
            out_ref[p, k * rank : (k + 1) * rank, :] = down_ref[k, :, p * piece : (p + 1) * piece]
        top, left = (p // halves) * group, (p % halves) * LANES
        out_ref[p, low:high, :] = jnp.concatenate(
            [up[top : top + group, left : left + LANES] for up in ups], axis=0
        ).astype(bf16)
        out_ref[p, high:, :] = marks


def packed(langs, table, down, up, holders):
    own_slots, rank, width = down.shape
    columns = up.shape[2]
    halves = columns // LANES
    payload = own_slots * (rank + rank * halves // holders) + 8
    steps = 1
    return pl.pallas_call(
        functools.partial(pack_kernel, halves),
        grid=(steps,),
        out_shape=jax.ShapeDtypeStruct((holders, payload, width // holders), bf16),
        in_specs=[
            pl.BlockSpec(langs.shape, lambda i: (0, 0)),
            pl.BlockSpec(table.shape, lambda i: (0, 0)),
            pl.BlockSpec((own_slots, rank, width // steps), lambda i: (0, 0, i)),
            pl.BlockSpec((own_slots, rank // steps, columns), lambda i: (0, i, 0)),
        ],
        out_specs=pl.BlockSpec(
            (holders // steps, payload, width // holders), lambda i: (i, 0, 0)
        ),
        compiler_params=pltpu.CompilerParams(vmem_limit_bytes=WIDE_LIMIT),
        name="packed_adapters",
    )(langs, table, down, up)


def weight_kernel(micro, quarters, first_ref, *refs):
    acts, cots = refs[:micro], refs[micro : micro + quarters]
    gathered_ref = refs[micro + quarters]
    outs, back_ref, held_ref, sems = refs[micro + quarters + 1 : -3], *refs[-3:]
    group = held_ref.shape[1]
    copies = []
    for k in range(quarters):
        quarter = lax.rem(first_ref[0] + k, quarters)
        copy = pltpu.make_async_copy(
            gathered_ref.at[pl.ds(quarter * group, group)], held_ref.at[k], sems.at[k]
        )
        copy.start()
        copies.append(copy)
    rows = jnp.concatenate([ref[0, 0] for ref in acts], axis=0)
    for k in range(quarters):
        copies[k].wait()
        weight = held_ref[k].reshape(-1, held_ref.shape[3])
        outs[k][...] = nt_dot(rows, weight).astype(bf16)
        back = jnp.dot(cots[(quarters - k) % quarters][...], weight, preferred_element_type=f32)
        if k == 0:
            back_ref[...] = back
        else:
            back_ref[...] += back


def weight_products(first, acts, cots, gathered):
    micro, quarters = len(acts), len(cots)
    holders, cols, width = gathered.shape
    rows = micro * BLOCK_ROWS
    group = holders // quarters
    results = pl.pallas_call(
        functools.partial(weight_kernel, micro, quarters),
        out_shape=(jax.ShapeDtypeStruct((rows, group * cols), bf16),) * quarters
        + (jax.ShapeDtypeStruct((rows, width), f32),),
        in_specs=[smem()]
        + [pl.BlockSpec(memory_space=pltpu.VMEM)] * (micro + quarters)
        + [pl.BlockSpec(memory_space=pltpu.HBM)],
        out_specs=(pl.BlockSpec(memory_space=pltpu.VMEM),) * (quarters + 1),
        scratch_shapes=[
            pltpu.VMEM((quarters, group, cols, width), bf16),
            pltpu.SemaphoreType.DMA((quarters,)),
        ],
        compiler_params=params(),
        cost_estimate=pl.CostEstimate(
            flops=4 * rows * width * cols * holders,
            bytes_accessed=2 * holders * cols * (width + 2 * rows) + 4 * rows * width,
            transcendentals=0,
        ),
        name="weight_products",
    )(first, *acts, *cots, gathered)
    return list(results[:-1]), results[-1]


def part_kernel(micro, second_ref, returned_ref, *refs):
    acts, parts_ref, up_ref = refs[:micro], refs[micro], refs[micro + 1]
    pieces, _, piece = second_ref.shape
    rank, columns = up_ref.shape[1:]
    halves = columns // LANES
    group = rank * halves // pieces
    for p in range(pieces):
        both = second_ref[p, micro * rank :, :].astype(f32)
        top, left = (p // halves) * group, (p % halves) * LANES
        for m in range(micro):
            up_ref[m, top : top + group, left : left + LANES] = both[m * group : (m + 1) * group]
    for m in range(micro):
        down = jnp.concatenate(
            [second_ref[p, m * rank : (m + 1) * rank, :] for p in range(pieces)], axis=1
        )
        parts = (
            nt_dot(down, acts[m][0, 0]).astype(bf16),
            nt_dot(up_ref[m].astype(bf16), returned_ref[m]).astype(bf16),
        )
        for q in range(parts_ref.shape[0]):
            for kind in range(2):
                parts_ref[q, kind, m] = parts[kind]


def rank_parts(second, returned, acts, rank, quarters):
    micro, _, columns = returned.shape
    return pl.pallas_call(
        functools.partial(part_kernel, micro),
        out_shape=(
            jax.ShapeDtypeStruct((quarters, 2, micro, rank, BLOCK_ROWS), bf16),
            jax.ShapeDtypeStruct((micro, rank, columns), f32),
        ),
        in_specs=[pl.BlockSpec(memory_space=pltpu.VMEM)] * (2 + micro),
        out_specs=(pl.BlockSpec(memory_space=pltpu.VMEM),) * 2,
        compiler_params=params(),
        name="rank_parts",
    )(second, returned, *acts)


def select_kernel(micro, own_slots, rank, slots_ref, first_ref, out_ref):
    holders = out_ref.shape[0]
    group = out_ref.shape[1] // micro - rank
    low = own_slots * rank
    for d in range(holders):
        ups = []
        for m in range(micro):
            slot = jnp.minimum(slots_ref[d * micro + m], holders * own_slots - 1)
            owner, k = slot // own_slots, slot % own_slots
            rows = pl.ds(pl.multiple_of(k * rank, rank), rank)
            out_ref[d, m * rank : (m + 1) * rank, :] = first_ref[owner, rows, :]
            held = first_ref[owner, low : low + own_slots * group, :].astype(f32)
            up = held[:group]
            for j in range(1, own_slots):
                up = jnp.where(k == j, held[j * group : (j + 1) * group], up)
            ups.append(up)
        out_ref[d, micro * rank :, :] = jnp.concatenate(ups, axis=0).astype(bf16)


def selected(slots, first, micro, own_slots, rank, group):
    holders, _, lanes = first.shape
    return pl.pallas_call(
        functools.partial(select_kernel, micro, own_slots, rank),
        out_shape=jax.ShapeDtypeStruct((holders, micro * (rank + group), lanes), bf16),
        in_specs=[smem(), pl.BlockSpec(memory_space=pltpu.VMEM)],
        out_specs=pl.BlockSpec(memory_space=pltpu.VMEM),
        compiler_params=params(),
        name="selected_pieces",
    )(slots, first)


def gradient_kernel(micro, live_ref, ranks_ref, down_ref, product_ref, out_ref):
    rank = ranks_ref.shape[1]
    pieces = down_ref.shape[0]
    for m in range(micro):
        back = (adapter_scale * ranks_ref[m].astype(f32)).T.astype(bf16)
        down = jnp.concatenate(
            [down_ref[p, m * rank : (m + 1) * rank, :] for p in range(pieces)], axis=1
        )
        lora = jnp.dot(back, down, preferred_element_type=f32).astype(bf16).astype(f32)
        part = product_ref[m * BLOCK_ROWS : (m + 1) * BLOCK_ROWS] + lora
        out_ref[m] = jnp.where(live_ref[m] > 0, part, 0.0).astype(bf16)


def input_gradients(live, ranks, second, product):
    micro, rank = ranks.shape[:2]
    rows, width = product.shape
    pieces, _, piece = second.shape
    steps = 2
    return pl.pallas_call(
        functools.partial(gradient_kernel, micro),
        grid=(steps,),
        out_shape=jax.ShapeDtypeStruct((micro, BLOCK_ROWS, width), bf16),
        in_specs=[
            smem(),
            pl.BlockSpec(ranks.shape, lambda i: (0, 0, 0)),
            pl.BlockSpec((pieces // steps, micro * rank, piece), lambda i: (i, 0, 0)),
            pl.BlockSpec((rows, width // steps), lambda i: (0, i)),
        ],
        out_specs=pl.BlockSpec((micro, BLOCK_ROWS, width // steps), lambda i: (0, 0, i)),
        compiler_params=pltpu.CompilerParams(vmem_limit_bytes=WIDE_LIMIT),
        cost_estimate=pl.CostEstimate(
            flops=2 * rows * width * rank, bytes_accessed=6 * rows * width, transcendentals=0
        ),
        name="input_gradients",
    )(live, ranks, second, product)


def layer_kernel(micro, live_ref, ranks_ref, up_ref, *refs):
    out_ref = refs[-1]
    for m in range(micro):
        total = adapter_scale * tn_dot(ranks_ref[m], up_ref[m].astype(bf16))
        for part_ref in refs[:-1]:
            total += part_ref[m * BLOCK_ROWS : (m + 1) * BLOCK_ROWS, :].astype(f32)
        out_ref[m] = jnp.where(live_ref[m] > 0, total, 0.0).astype(bf16)


def layer_outputs(live, ranks, up, parts):
    micro, _, columns = up.shape
    return pl.pallas_call(
        functools.partial(layer_kernel, micro),
        out_shape=jax.ShapeDtypeStruct((micro, BLOCK_ROWS, columns), bf16),
        in_specs=[smem()] + [pl.BlockSpec(memory_space=pltpu.VMEM)] * (2 + len(parts)),
        out_specs=pl.BlockSpec(memory_space=pltpu.VMEM),
        compiler_params=params(),
        name="layer_outputs",
    )(live, ranks, up, *parts)


def rank_kernel(parts_ref, incoming_ref, ranks_ref, pieces_ref):
    micro, rank = parts_ref.shape[2:4]
    total = parts_ref[0].astype(f32)
    for q in range(1, parts_ref.shape[0]):
        total += parts_ref[q].astype(f32)
    ranks_ref[...] = total.astype(bf16)
    half = rank // 2
    for m in range(micro):
        grad = jnp.dot(ranks_ref[0, m], incoming_ref[m], preferred_element_type=f32)
        grad = (grad * (adapter_scale / BLOCK_ROWS)).astype(bf16)
        for p in range(pieces_ref.shape[0]):
            top = (p % 2) * half
            pieces_ref[p, m] = grad[top : top + half]


def ranks_and_pieces(parts, incoming, holders):
    micro, rank = parts.shape[2:4]
    columns = incoming.shape[2]
    return pl.pallas_call(
        rank_kernel,
        out_shape=(
            jax.ShapeDtypeStruct(parts.shape[1:], bf16),
            jax.ShapeDtypeStruct((holders, micro, rank // 2, columns), bf16),
        ),
        in_specs=[pl.BlockSpec(memory_space=pltpu.VMEM)] * 2,
        out_specs=(pl.BlockSpec(memory_space=pltpu.VMEM),) * 2,
        compiler_params=params(),
        name="ranks_and_pieces",
    )(parts, incoming)


def slot_kernel(marks_ref, first_ref, pieces_ref, out_ref):
    holders, micro = pieces_ref.shape[:2]
    for i in range(out_ref.shape[0]):
        total, square = None, None
        for d in range(holders):
            partial = None
            for m in range(micro):
                hit = marks_ref[d * micro + m] == first_ref[0] + i
                term = jnp.where(hit, pieces_ref[d, m].astype(f32), 0.0)
                partial = term if partial is None else partial + term
            total = partial if total is None else total + partial
            squared = partial * partial
            square = squared if square is None else square + squared
        out_ref[i, 0] = total
        out_ref[i, 1] = square


def slot_sums(marks, first_slot, pieces, own_slots):
    return pl.pallas_call(
        slot_kernel,
        out_shape=jax.ShapeDtypeStruct((own_slots, 2) + pieces.shape[2:], f32),
        in_specs=[smem(), smem(), pl.BlockSpec(memory_space=pltpu.VMEM)],
        out_specs=pl.BlockSpec(memory_space=pltpu.VMEM),
        compiler_params=params(),
        name="slot_sums",
    )(marks, first_slot, pieces)


def place_kernel(core_ref, own_ref, other_ref, sum_ref, square_ref):
    half = own_ref.shape[2]
    low = core_ref[0] == 0
    for k in range(own_ref.shape[0]):
        for kind, out_ref in enumerate((sum_ref, square_ref)):
            own, other = own_ref[k, kind], other_ref[k, kind]
            out_ref[k, :half] = jnp.where(low, own, other)
            out_ref[k, half:] = jnp.where(low, other, own)


def placed(core, own, other):
    own_slots, _, half, columns = own.shape
    shape = jax.ShapeDtypeStruct((own_slots, 2 * half, columns), f32)
    return pl.pallas_call(
        place_kernel,
        out_shape=(shape, shape),
        in_specs=[smem()] + [pl.BlockSpec(memory_space=pltpu.VMEM)] * 2,
        out_specs=(pl.BlockSpec(memory_space=pltpu.VMEM),) * 2,
        compiler_params=params(),
        name="placed_sums",
    )(core, own, other)


def shards(
    activations, cotangent, base_weight, adapter_down, adapter_up, slot_language, block_language
):
    holders = lax.axis_size("dp")
    quarters = lax.axis_size("mp")
    own_slots, width, rank = adapter_down.shape[1:]
    columns = adapter_up.shape[3]
    micro = activations.shape[1]
    rows = micro * BLOCK_ROWS
    piece = width // holders
    up_groups = holders // (columns // LANES)
    up_rows = rank // up_groups
    me = lax.axis_index("dp")

    returned = passed_along(cotangent, "section", -1)[0]
    arrived = [passed_along(activations[:, m : m + 1], "section", 1) for m in range(micro)]

    slot_table = slot_language[0]
    langs = block_language[0, :, 0]
    live = (langs < slot_table.shape[0]).astype(jnp.int32)

    weight = jnp.swapaxes(base_weight[0], 0, 1)
    gathered = lax.all_gather(weight, "dp", axis=0)
    flat_cots = returned.reshape(rows, columns)
    cots = [flat_cots] + [
        lax.ppermute(flat_cots, "mp", [(i, (i + k) % quarters) for i in range(quarters)])
        for k in range(1, quarters)
    ]

    down = jnp.swapaxes(adapter_down[0], 1, 2)
    first = packed(langs[None, :], slot_language, down, adapter_up[0], holders)
    first = exchanged(first, "dp")

    marked = own_slots * (rank + up_rows)
    slots = first[:, marked : marked + micro, 0].astype(jnp.int32).reshape(-1)
    second = selected(slots, first, micro, own_slots, rank, up_rows)
    second, arrived[0], cots[1] = lax.optimization_barrier((second, arrived[0], cots[1]))
    second = exchanged(second, "dp")
    second, cots = lax.optimization_barrier((second, cots))

    parts, up = rank_parts(second, returned, arrived, rank, quarters)
    parts = exchanged(parts, "mp")
    quarter = lax.axis_index("mp").astype(jnp.int32).reshape(1)
    base_parts, back = weight_products(quarter, arrived, cots, gathered)
    parts, base_parts = lax.optimization_barrier((parts, base_parts))
    ranks, pieces = ranks_and_pieces(parts, returned, holders)
    rank_in, rank_back = ranks[0], ranks[1]

    pieces = exchanged(pieces, "dp")
    base_parts = [base_parts[0]] + [
        lax.ppermute(base_parts[k], "mp", [(i, (i + k) % quarters) for i in range(quarters)])
        for k in range(1, quarters)
    ]
    layer_out = layer_outputs(live, rank_in, up, base_parts)[None]
    input_gradient = input_gradients(live, rank_back, second, back)[None]
    pieces, input_gradient, layer_out = lax.optimization_barrier(
        (pieces, input_gradient, layer_out)
    )
    other = slot_sums(slots, (own_slots * (me ^ 1)).astype(jnp.int32).reshape(1), pieces, own_slots)
    other = lax.ppermute(other, "dp", [(i, i ^ 1) for i in range(holders)])
    own = slot_sums(slots, (own_slots * me).astype(jnp.int32).reshape(1), pieces, own_slots)
    grad_sum, grad_square = placed((me % 2).astype(jnp.int32).reshape(1), own, other)

    return (layer_out, input_gradient, grad_sum[None], grad_square[None])


def solution(mesh):
    in_specs = (
        P("section", None, "dp", "mp"),
        P("section", None, "dp", "mp"),
        P("section", "mp", "dp"),
        P("section", "dp", "mp", None),
        P("section", "dp", None, "mp"),
        P("section", None),
        P("section", None, "dp"),
    )
    out_specs = (
        P("section", None, "dp", "mp"),
        P("section", None, "dp", "mp"),
        P("section", "dp", None, "mp"),
        P("section", "dp", None, "mp"),
    )
    return jax.shard_map(shards, mesh=mesh, in_specs=in_specs, out_specs=out_specs, check_vma=False)
```

```python
import functools

import jax
import jax.numpy as jnp
from jax import lax
from jax.experimental import pallas as pl
from jax.experimental.pallas import tpu as pltpu
from jax.sharding import PartitionSpec as P

BLOCK_ROWS = 128
LANES = 128

adapter_scale = 2.0

bf16, f32 = jnp.bfloat16, jnp.float32
VMEM_LIMIT = 24 * 1024 * 1024
WIDE_LIMIT = 60 * 1024 * 1024


def passed_along(array, axis, by):
    devices = lax.axis_size(axis)
    return lax.ppermute(array, axis, [(i, (i + by) % devices) for i in range(devices)])


def exchanged(array, axis):
    return lax.all_to_all(array, axis, split_axis=0, concat_axis=0, tiled=True)


def smem():
    return pl.BlockSpec(memory_space=pltpu.SMEM)


def params():
    return pltpu.CompilerParams(vmem_limit_bytes=VMEM_LIMIT)


def nt_dot(a, b):
    return lax.dot_general(a, b, (((1,), (1,)), ((), ())), preferred_element_type=f32)


def tn_dot(a, b):
    return lax.dot_general(a, b, (((0,), (0,)), ((), ())), preferred_element_type=f32)


def pack_kernel(halves, langs_ref, table_ref, down_ref, up_ref, out_ref):
    pieces, payload, piece = out_ref.shape
    own_slots, rank, _ = down_ref.shape
    micro, count = langs_ref.shape[1], table_ref.shape[1]
    group = up_ref.shape[1] * halves // pieces
    low, high = own_slots * rank, own_slots * (rank + group)
    lane = lax.broadcasted_iota(jnp.int32, (1, count), 1)
    row = lax.broadcasted_iota(jnp.int32, (payload - high, piece), 0)
    marks = jnp.zeros((payload - high, piece), f32)
    for m in range(micro):
        match = table_ref[...] == langs_ref[:, m : m + 1]
        slot = jnp.min(jnp.where(match, lane, count), axis=1, keepdims=True).astype(f32)
        marks = jnp.where(row == m, slot, marks)
    marks = marks.astype(bf16)
    ups = [up_ref[k].astype(f32) for k in range(own_slots)]
    for p in range(pieces):
        for k in range(own_slots):
            out_ref[p, k * rank : (k + 1) * rank, :] = down_ref[k, :, p * piece : (p + 1) * piece]
        top, left = (p // halves) * group, (p % halves) * LANES
        out_ref[p, low:high, :] = jnp.concatenate(
            [up[top : top + group, left : left + LANES] for up in ups], axis=0
        ).astype(bf16)
        out_ref[p, high:, :] = marks


def packed(langs, table, down, up, holders):
    own_slots, rank, width = down.shape
    columns = up.shape[2]
    halves = columns // LANES
    payload = own_slots * (rank + rank * halves // holders) + 8
    steps = 1
    return pl.pallas_call(
        functools.partial(pack_kernel, halves),
        grid=(steps,),
        out_shape=jax.ShapeDtypeStruct((holders, payload, width // holders), bf16),
        in_specs=[
            pl.BlockSpec(langs.shape, lambda i: (0, 0)),
            pl.BlockSpec(table.shape, lambda i: (0, 0)),
            pl.BlockSpec((own_slots, rank, width // steps), lambda i: (0, 0, i)),
            pl.BlockSpec((own_slots, rank // steps, columns), lambda i: (0, i, 0)),
        ],
        out_specs=pl.BlockSpec(
            (holders // steps, payload, width // holders), lambda i: (i, 0, 0)
        ),
        compiler_params=pltpu.CompilerParams(vmem_limit_bytes=WIDE_LIMIT),
        name="packed_adapters",
    )(langs, table, down, up)


def weight_kernel(micro, quarters, first_ref, *refs):
    acts, cots = refs[:micro], refs[micro : micro + quarters]
    gathered_ref = refs[micro + quarters]
    outs, back_ref = refs[micro + quarters + 1 : -1], refs[-1]
    holders, _, width = gathered_ref.shape
    group = holders // quarters
    rows = jnp.concatenate([ref[0, 0] for ref in acts], axis=0)
    for k in range(quarters):
        quarter = lax.rem(first_ref[0] + k, quarters)
        weight = gathered_ref[pl.ds(quarter * group, group)].reshape(-1, width)
        outs[k][...] = nt_dot(rows, weight).astype(bf16)
        back = jnp.dot(cots[(quarters - k) % quarters][...], weight, preferred_element_type=f32)
        if k == 0:
            back_ref[...] = back
        else:
            back_ref[...] += back


def weight_products(first, acts, cots, gathered):
    micro, quarters = len(acts), len(cots)
    holders, cols, width = gathered.shape
    rows = micro * BLOCK_ROWS
    group = holders // quarters
    results = pl.pallas_call(
        functools.partial(weight_kernel, micro, quarters),
        out_shape=(jax.ShapeDtypeStruct((rows, group * cols), bf16),) * quarters
        + (jax.ShapeDtypeStruct((rows, width), f32),),
        in_specs=[smem()] + [pl.BlockSpec(memory_space=pltpu.VMEM)] * (micro + quarters + 1),
        out_specs=(pl.BlockSpec(memory_space=pltpu.VMEM),) * (quarters + 1),
        compiler_params=pltpu.CompilerParams(vmem_limit_bytes=VMEM_LIMIT),
        cost_estimate=pl.CostEstimate(
            flops=4 * rows * width * cols * holders,
            bytes_accessed=2 * holders * cols * (width + 2 * rows) + 4 * rows * width,
            transcendentals=0,
        ),
        name="weight_products",
    )(first, *acts, *cots, gathered)
    return list(results[:-1]), results[-1]


def part_kernel(micro, second_ref, returned_ref, *refs):
    acts, parts_ref, up_ref = refs[:micro], refs[micro], refs[micro + 1]
    pieces, _, piece = second_ref.shape
    rank, columns = up_ref.shape[1:]
    halves = columns // LANES
    group = rank * halves // pieces
    for p in range(pieces):
        both = second_ref[p, micro * rank :, :].astype(f32)
        top, left = (p // halves) * group, (p % halves) * LANES
        for m in range(micro):
            up_ref[m, top : top + group, left : left + LANES] = both[m * group : (m + 1) * group]
    for m in range(micro):
        down = jnp.concatenate(
            [second_ref[p, m * rank : (m + 1) * rank, :] for p in range(pieces)], axis=1
        )
        parts = (
            nt_dot(down, acts[m][0, 0]).astype(bf16),
            nt_dot(up_ref[m].astype(bf16), returned_ref[m]).astype(bf16),
        )
        for q in range(parts_ref.shape[0]):
            for kind in range(2):
                parts_ref[q, kind, m] = parts[kind]


def rank_parts(second, returned, acts, rank, quarters):
    micro, _, columns = returned.shape
    return pl.pallas_call(
        functools.partial(part_kernel, micro),
        out_shape=(
            jax.ShapeDtypeStruct((quarters, 2, micro, rank, BLOCK_ROWS), bf16),
            jax.ShapeDtypeStruct((micro, rank, columns), f32),
        ),
        in_specs=[pl.BlockSpec(memory_space=pltpu.VMEM)] * (2 + micro),
        out_specs=(pl.BlockSpec(memory_space=pltpu.VMEM),) * 2,
        compiler_params=params(),
        name="rank_parts",
    )(second, returned, *acts)


def select_kernel(micro, own_slots, rank, slots_ref, first_ref, out_ref):
    holders = out_ref.shape[0]
    group = out_ref.shape[1] // micro - rank
    low = own_slots * rank
    for d in range(holders):
        ups = []
        for m in range(micro):
            slot = jnp.minimum(slots_ref[d * micro + m], holders * own_slots - 1)
            owner, k = slot // own_slots, slot % own_slots
            rows = pl.ds(pl.multiple_of(k * rank, rank), rank)
            out_ref[d, m * rank : (m + 1) * rank, :] = first_ref[owner, rows, :]
            held = first_ref[owner, low : low + own_slots * group, :].astype(f32)
            up = held[:group]
            for j in range(1, own_slots):
                up = jnp.where(k == j, held[j * group : (j + 1) * group], up)
            ups.append(up)
        out_ref[d, micro * rank :, :] = jnp.concatenate(ups, axis=0).astype(bf16)


def selected(slots, first, micro, own_slots, rank, group):
    holders, _, lanes = first.shape
    return pl.pallas_call(
        functools.partial(select_kernel, micro, own_slots, rank),
        out_shape=jax.ShapeDtypeStruct((holders, micro * (rank + group), lanes), bf16),
        in_specs=[smem(), pl.BlockSpec(memory_space=pltpu.VMEM)],
        out_specs=pl.BlockSpec(memory_space=pltpu.VMEM),
        compiler_params=params(),
        name="selected_pieces",
    )(slots, first)


def gradient_kernel(micro, live_ref, ranks_ref, down_ref, product_ref, out_ref):
    rank = ranks_ref.shape[1]
    pieces = down_ref.shape[0]
    for m in range(micro):
        back = (adapter_scale * ranks_ref[m].astype(f32)).T.astype(bf16)
        down = jnp.concatenate(
            [down_ref[p, m * rank : (m + 1) * rank, :] for p in range(pieces)], axis=1
        )
        lora = jnp.dot(back, down, preferred_element_type=f32).astype(bf16).astype(f32)
        part = product_ref[m * BLOCK_ROWS : (m + 1) * BLOCK_ROWS] + lora
        out_ref[m] = jnp.where(live_ref[m] > 0, part, 0.0).astype(bf16)


def input_gradients(live, ranks, second, product):
    micro, rank = ranks.shape[:2]
    rows, width = product.shape
    pieces, _, piece = second.shape
    steps = 2
    return pl.pallas_call(
        functools.partial(gradient_kernel, micro),
        grid=(steps,),
        out_shape=jax.ShapeDtypeStruct((micro, BLOCK_ROWS, width), bf16),
        in_specs=[
            smem(),
            pl.BlockSpec(ranks.shape, lambda i: (0, 0, 0)),
            pl.BlockSpec((pieces // steps, micro * rank, piece), lambda i: (i, 0, 0)),
            pl.BlockSpec((rows, width // steps), lambda i: (0, i)),
        ],
        out_specs=pl.BlockSpec((micro, BLOCK_ROWS, width // steps), lambda i: (0, 0, i)),
        compiler_params=pltpu.CompilerParams(vmem_limit_bytes=WIDE_LIMIT),
        cost_estimate=pl.CostEstimate(
            flops=2 * rows * width * rank, bytes_accessed=6 * rows * width, transcendentals=0
        ),
        name="input_gradients",
    )(live, ranks, second, product)


def layer_kernel(micro, live_ref, ranks_ref, up_ref, *refs):
    out_ref = refs[-1]
    for m in range(micro):
        total = adapter_scale * tn_dot(ranks_ref[m], up_ref[m].astype(bf16))
        for part_ref in refs[:-1]:
            total += part_ref[m * BLOCK_ROWS : (m + 1) * BLOCK_ROWS, :].astype(f32)
        out_ref[m] = jnp.where(live_ref[m] > 0, total, 0.0).astype(bf16)


def layer_outputs(live, ranks, up, parts):
    micro, _, columns = up.shape
    return pl.pallas_call(
        functools.partial(layer_kernel, micro),
        out_shape=jax.ShapeDtypeStruct((micro, BLOCK_ROWS, columns), bf16),
        in_specs=[smem()] + [pl.BlockSpec(memory_space=pltpu.VMEM)] * (2 + len(parts)),
        out_specs=pl.BlockSpec(memory_space=pltpu.VMEM),
        compiler_params=params(),
        name="layer_outputs",
    )(live, ranks, up, *parts)


def rank_kernel(parts_ref, incoming_ref, ranks_ref, pieces_ref):
    micro, rank = parts_ref.shape[2:4]
    total = parts_ref[0].astype(f32)
    for q in range(1, parts_ref.shape[0]):
        total += parts_ref[q].astype(f32)
    ranks_ref[...] = total.astype(bf16)
    half = rank // 2
    for m in range(micro):
        grad = jnp.dot(ranks_ref[0, m], incoming_ref[m], preferred_element_type=f32)
        grad = (grad * (adapter_scale / BLOCK_ROWS)).astype(bf16)
        for p in range(pieces_ref.shape[0]):
            top = (p % 2) * half
            pieces_ref[p, m] = grad[top : top + half]


def ranks_and_pieces(parts, incoming, holders):
    micro, rank = parts.shape[2:4]
    columns = incoming.shape[2]
    return pl.pallas_call(
        rank_kernel,
        out_shape=(
            jax.ShapeDtypeStruct(parts.shape[1:], bf16),
            jax.ShapeDtypeStruct((holders, micro, rank // 2, columns), bf16),
        ),
        in_specs=[pl.BlockSpec(memory_space=pltpu.VMEM)] * 2,
        out_specs=(pl.BlockSpec(memory_space=pltpu.VMEM),) * 2,
        compiler_params=params(),
        name="ranks_and_pieces",
    )(parts, incoming)


def slot_kernel(marks_ref, first_ref, pieces_ref, out_ref):
    holders, micro = pieces_ref.shape[:2]
    for i in range(out_ref.shape[0]):
        total, square = None, None
        for d in range(holders):
            partial = None
            for m in range(micro):
                hit = marks_ref[d * micro + m] == first_ref[0] + i
                term = jnp.where(hit, pieces_ref[d, m].astype(f32), 0.0)
                partial = term if partial is None else partial + term
            total = partial if total is None else total + partial
            squared = partial * partial
            square = squared if square is None else square + squared
        out_ref[i, 0] = total
        out_ref[i, 1] = square


def slot_sums(marks, first_slot, pieces, own_slots):
    return pl.pallas_call(
        slot_kernel,
        out_shape=jax.ShapeDtypeStruct((own_slots, 2) + pieces.shape[2:], f32),
        in_specs=[smem(), smem(), pl.BlockSpec(memory_space=pltpu.VMEM)],
        out_specs=pl.BlockSpec(memory_space=pltpu.VMEM),
        compiler_params=params(),
        name="slot_sums",
    )(marks, first_slot, pieces)


def place_kernel(core_ref, own_ref, other_ref, sum_ref, square_ref):
    half = own_ref.shape[2]
    low = core_ref[0] == 0
    for k in range(own_ref.shape[0]):
        for kind, out_ref in enumerate((sum_ref, square_ref)):
            own, other = own_ref[k, kind], other_ref[k, kind]
            out_ref[k, :half] = jnp.where(low, own, other)
            out_ref[k, half:] = jnp.where(low, other, own)


def placed(core, own, other):
    own_slots, _, half, columns = own.shape
    shape = jax.ShapeDtypeStruct((own_slots, 2 * half, columns), f32)
    return pl.pallas_call(
        place_kernel,
        out_shape=(shape, shape),
        in_specs=[smem()] + [pl.BlockSpec(memory_space=pltpu.VMEM)] * 2,
        out_specs=(pl.BlockSpec(memory_space=pltpu.VMEM),) * 2,
        compiler_params=params(),
        name="placed_sums",
    )(core, own, other)


def shards(
    activations, cotangent, base_weight, adapter_down, adapter_up, slot_language, block_language
):
    holders = lax.axis_size("dp")
    quarters = lax.axis_size("mp")
    own_slots, width, rank = adapter_down.shape[1:]
    columns = adapter_up.shape[3]
    micro = activations.shape[1]
    rows = micro * BLOCK_ROWS
    piece = width // holders
    up_groups = holders // (columns // LANES)
    up_rows = rank // up_groups
    me = lax.axis_index("dp")

    returned = passed_along(cotangent, "section", -1)[0]
    arrived = [passed_along(activations[:, m : m + 1], "section", 1) for m in range(micro)]

    slot_table = slot_language[0]
    langs = block_language[0, :, 0]
    live = (langs < slot_table.shape[0]).astype(jnp.int32)

    weight = jnp.swapaxes(base_weight[0], 0, 1)
    gathered = lax.all_gather(weight, "dp", axis=0)
    flat_cots = returned.reshape(rows, columns)
    cots = [flat_cots] + [
        lax.ppermute(flat_cots, "mp", [(i, (i + k) % quarters) for i in range(quarters)])
        for k in range(1, quarters)
    ]

    down = jnp.swapaxes(adapter_down[0], 1, 2)
    first = packed(langs[None, :], slot_language, down, adapter_up[0], holders)
    first = exchanged(first, "dp")

    marked = own_slots * (rank + up_rows)
    slots = first[:, marked : marked + micro, 0].astype(jnp.int32).reshape(-1)
    second = selected(slots, first, micro, own_slots, rank, up_rows)
    second, arrived[0], cots[1] = lax.optimization_barrier((second, arrived[0], cots[1]))
    second = exchanged(second, "dp")
    second, cots = lax.optimization_barrier((second, cots))

    parts, up = rank_parts(second, returned, arrived, rank, quarters)
    parts = exchanged(parts, "mp")
    quarter = lax.axis_index("mp").astype(jnp.int32).reshape(1)
    base_parts, back = weight_products(quarter, arrived, cots, gathered)
    parts, base_parts = lax.optimization_barrier((parts, base_parts))
    ranks, pieces = ranks_and_pieces(parts, returned, holders)
    rank_in, rank_back = ranks[0], ranks[1]

    pieces = exchanged(pieces, "dp")
    base_parts = [base_parts[0]] + [
        lax.ppermute(base_parts[k], "mp", [(i, (i + k) % quarters) for i in range(quarters)])
        for k in range(1, quarters)
    ]
    layer_out = layer_outputs(live, rank_in, up, base_parts)[None]
    input_gradient = input_gradients(live, rank_back, second, back)[None]
    pieces, input_gradient, layer_out = lax.optimization_barrier(
        (pieces, input_gradient, layer_out)
    )
    other = slot_sums(slots, (own_slots * (me ^ 1)).astype(jnp.int32).reshape(1), pieces, own_slots)
    other = lax.ppermute(other, "dp", [(i, i ^ 1) for i in range(holders)])
    own = slot_sums(slots, (own_slots * me).astype(jnp.int32).reshape(1), pieces, own_slots)
    grad_sum, grad_square = placed((me % 2).astype(jnp.int32).reshape(1), own, other)

    return (layer_out, input_gradient, grad_sum[None], grad_square[None])


def solution(mesh):
    in_specs = (
        P("section", None, "dp", "mp"),
        P("section", None, "dp", "mp"),
        P("section", "mp", "dp"),
        P("section", "dp", "mp", None),
        P("section", "dp", None, "mp"),
        P("section", None),
        P("section", None, "dp"),
    )
    out_specs = (
        P("section", None, "dp", "mp"),
        P("section", None, "dp", "mp"),
        P("section", "dp", None, "mp"),
        P("section", "dp", None, "mp"),
    )
    return jax.shard_map(shards, mesh=mesh, in_specs=in_specs, out_specs=out_specs, check_vma=False)
```

```python
import functools

import jax
import jax.numpy as jnp
from jax import lax
from jax.experimental import pallas as pl
from jax.experimental.pallas import tpu as pltpu
from jax.sharding import PartitionSpec as P

BLOCK_ROWS = 128
LANES = 128

adapter_scale = 2.0

bf16, f32 = jnp.bfloat16, jnp.float32
VMEM_LIMIT = 24 * 1024 * 1024
WIDE_LIMIT = 60 * 1024 * 1024
PARTS = 4


def passed_along(array, axis, by):
    devices = lax.axis_size(axis)
    return lax.ppermute(array, axis, [(i, (i + by) % devices) for i in range(devices)])


def exchanged(array, axis):
    return lax.all_to_all(array, axis, split_axis=0, concat_axis=0, tiled=True)


def smem():
    return pl.BlockSpec(memory_space=pltpu.SMEM)


def params():
    return pltpu.CompilerParams(vmem_limit_bytes=VMEM_LIMIT)


def nt_dot(a, b):
    return lax.dot_general(a, b, (((1,), (1,)), ((), ())), preferred_element_type=f32)


def tn_dot(a, b):
    return lax.dot_general(a, b, (((0,), (0,)), ((), ())), preferred_element_type=f32)


def started(source, target, sem):
    copy = pltpu.make_async_copy(source, target, sem)
    copy.start()
    return copy


def pack_kernel(
    halves,
    langs_in,
    table_in,
    down_in,
    up_in,
    out,
    langs_ref,
    table_ref,
    down_ref,
    up_ref,
    out_ref,
    in_sems,
    out_sems,
):
    pieces, payload, piece = out_ref.shape
    own_slots, rank, width = down_ref.shape
    micro, count = langs_ref.shape[1], table_ref.shape[1]
    group = rank * halves // pieces
    low, high = own_slots * rank, own_slots * (rank + group)
    span, chunk = width // PARTS, pieces // PARTS
    small = [
        started(langs_in, langs_ref, in_sems.at[0]),
        started(table_in, table_ref, in_sems.at[1]),
        started(up_in, up_ref, in_sems.at[2]),
    ]
    large = []
    for i in range(PARTS):
        columns = pl.ds(i * span, span)
        large.append(
            started(
                down_in.at[:, :, columns], down_ref.at[:, :, columns], in_sems.at[3 + i]
            )
        )
    for copy in small:
        copy.wait()
    lane = lax.broadcasted_iota(jnp.int32, (1, count), 1)
    row = lax.broadcasted_iota(jnp.int32, (payload - high, piece), 0)
    marks = jnp.zeros((payload - high, piece), f32)
    for m in range(micro):
        match = table_ref[...] == langs_ref[:, m : m + 1]
        slot = jnp.min(jnp.where(match, lane, count), axis=1, keepdims=True).astype(f32)
        marks = jnp.where(row == m, slot, marks)
    marks = marks.astype(bf16)
    ups = [up_ref[k].astype(f32) for k in range(own_slots)]
    sent = []
    for i in range(PARTS):
        large[i].wait()
        for p in range(i * chunk, (i + 1) * chunk):
            for k in range(own_slots):
                out_ref[p, k * rank : (k + 1) * rank, :] = down_ref[
                    k, :, p * piece : (p + 1) * piece
                ]
            top, left = (p // halves) * group, (p % halves) * LANES
            out_ref[p, low:high, :] = jnp.concatenate(
                [up[top : top + group, left : left + LANES] for up in ups], axis=0
            ).astype(bf16)
            out_ref[p, high:, :] = marks
        some = pl.ds(i * chunk, chunk)
        sent.append(started(out_ref.at[some], out.at[some], out_sems.at[i]))
    for copy in sent:
        copy.wait()


def packed(langs, table, down, up, holders):
    own_slots, rank, width = down.shape
    halves = up.shape[2] // LANES
    payload = own_slots * (rank + rank * halves // holders) + 8
    out = (holders, payload, width // holders)
    return pl.pallas_call(
        functools.partial(pack_kernel, halves),
        out_shape=jax.ShapeDtypeStruct(out, bf16),
        in_specs=[pl.BlockSpec(memory_space=pl.ANY)] * 4,
        out_specs=pl.BlockSpec(memory_space=pl.ANY),
        scratch_shapes=[
            pltpu.VMEM(langs.shape, jnp.int32),
            pltpu.VMEM(table.shape, jnp.int32),
            pltpu.VMEM(down.shape, bf16),
            pltpu.VMEM(up.shape, bf16),
            pltpu.VMEM(out, bf16),
            pltpu.SemaphoreType.DMA((3 + PARTS,)),
            pltpu.SemaphoreType.DMA((PARTS,)),
        ],
        compiler_params=pltpu.CompilerParams(vmem_limit_bytes=WIDE_LIMIT),
        name="packed_adapters",
    )(langs, table, down, up)


def weight_kernel(micro, quarters, first_ref, *refs):
    acts, cots = refs[:micro], refs[micro : micro + quarters]
    gathered_ref = refs[micro + quarters]
    outs, back_ref = refs[micro + quarters + 1 : -1], refs[-1]
    holders, _, width = gathered_ref.shape
    group = holders // quarters
    rows = jnp.concatenate([ref[0, 0] for ref in acts], axis=0)
    for k in range(quarters):
        quarter = lax.rem(first_ref[0] + k, quarters)
        weight = gathered_ref[pl.ds(quarter * group, group)].reshape(-1, width)
        outs[k][...] = nt_dot(rows, weight).astype(bf16)
        back = jnp.dot(cots[(quarters - k) % quarters][...], weight, preferred_element_type=f32)
        if k == 0:
            back_ref[...] = back
        else:
            back_ref[...] += back


def weight_products(first, acts, cots, gathered):
    micro, quarters = len(acts), len(cots)
    holders, cols, width = gathered.shape
    rows = micro * BLOCK_ROWS
    group = holders // quarters
    results = pl.pallas_call(
        functools.partial(weight_kernel, micro, quarters),
        out_shape=(jax.ShapeDtypeStruct((rows, group * cols), bf16),) * quarters
        + (jax.ShapeDtypeStruct((rows, width), f32),),
        in_specs=[smem()] + [pl.BlockSpec(memory_space=pltpu.VMEM)] * (micro + quarters + 1),
        out_specs=(pl.BlockSpec(memory_space=pltpu.VMEM),) * (quarters + 1),
        compiler_params=pltpu.CompilerParams(vmem_limit_bytes=VMEM_LIMIT),
        cost_estimate=pl.CostEstimate(
            flops=4 * rows * width * cols * holders,
            bytes_accessed=2 * holders * cols * (width + 2 * rows) + 4 * rows * width,
            transcendentals=0,
        ),
        name="weight_products",
    )(first, *acts, *cots, gathered)
    return list(results[:-1]), results[-1]


def part_kernel(micro, second_ref, returned_ref, *refs):
    acts, parts_ref, up_ref = refs[:micro], refs[micro], refs[micro + 1]
    pieces, _, piece = second_ref.shape
    rank, columns = up_ref.shape[1:]
    halves = columns // LANES
    group = rank * halves // pieces
    for p in range(pieces):
        both = second_ref[p, micro * rank :, :].astype(f32)
        top, left = (p // halves) * group, (p % halves) * LANES
        for m in range(micro):
            up_ref[m, top : top + group, left : left + LANES] = both[m * group : (m + 1) * group]
    for m in range(micro):
        down = jnp.concatenate(
            [second_ref[p, m * rank : (m + 1) * rank, :] for p in range(pieces)], axis=1
        )
        parts = (
            nt_dot(down, acts[m][0, 0]).astype(bf16),
            nt_dot(up_ref[m].astype(bf16), returned_ref[m]).astype(bf16),
        )
        for q in range(parts_ref.shape[0]):
            for kind in range(2):
                parts_ref[q, kind, m] = parts[kind]


def rank_parts(second, returned, acts, rank, quarters):
    micro, _, columns = returned.shape
    return pl.pallas_call(
        functools.partial(part_kernel, micro),
        out_shape=(
            jax.ShapeDtypeStruct((quarters, 2, micro, rank, BLOCK_ROWS), bf16),
            jax.ShapeDtypeStruct((micro, rank, columns), f32),
        ),
        in_specs=[pl.BlockSpec(memory_space=pltpu.VMEM)] * (2 + micro),
        out_specs=(pl.BlockSpec(memory_space=pltpu.VMEM),) * 2,
        compiler_params=params(),
        name="rank_parts",
    )(second, returned, *acts)


def select_kernel(micro, own_slots, rank, slots_ref, first_ref, out, out_ref, sems):
    holders = out_ref.shape[0]
    group = out_ref.shape[1] // micro - rank
    low = own_slots * rank
    chunk = holders // PARTS
    sent = []
    for i in range(PARTS):
        for d in range(i * chunk, (i + 1) * chunk):
            ups = []
            for m in range(micro):
                slot = jnp.minimum(slots_ref[d * micro + m], holders * own_slots - 1)
                owner, k = lax.div(slot, own_slots), lax.rem(slot, own_slots)
                rows = pl.ds(pl.multiple_of(k * rank, rank), rank)
                out_ref[d, m * rank : (m + 1) * rank, :] = first_ref[owner, rows, :]
                held = first_ref[owner, low : low + own_slots * group, :].astype(f32)
                up = held[:group]
                for j in range(1, own_slots):
                    up = jnp.where(k == j, held[j * group : (j + 1) * group], up)
                ups.append(up)
            out_ref[d, micro * rank :, :] = jnp.concatenate(ups, axis=0).astype(bf16)
        some = pl.ds(i * chunk, chunk)
        sent.append(started(out_ref.at[some], out.at[some], sems.at[i]))
    for copy in sent:
        copy.wait()


def selected(slots, first, micro, own_slots, rank, group):
    holders, _, lanes = first.shape
    out = (holders, micro * (rank + group), lanes)
    return pl.pallas_call(
        functools.partial(select_kernel, micro, own_slots, rank),
        out_shape=jax.ShapeDtypeStruct(out, bf16),
        in_specs=[smem(), pl.BlockSpec(memory_space=pltpu.VMEM)],
        out_specs=pl.BlockSpec(memory_space=pl.ANY),
        scratch_shapes=[pltpu.VMEM(out, bf16), pltpu.SemaphoreType.DMA((PARTS,))],
        compiler_params=params(),
        name="selected_pieces",
    )(slots, first)


def gradient_kernel(micro, live_ref, ranks_ref, down_ref, product_ref, out_ref):
    rank = ranks_ref.shape[1]
    pieces = down_ref.shape[0]
    for m in range(micro):
        back = (adapter_scale * ranks_ref[m].astype(f32)).T.astype(bf16)
        down = jnp.concatenate(
            [down_ref[p, m * rank : (m + 1) * rank, :] for p in range(pieces)], axis=1
        )
        lora = jnp.dot(back, down, preferred_element_type=f32).astype(bf16).astype(f32)
        part = product_ref[m * BLOCK_ROWS : (m + 1) * BLOCK_ROWS] + lora
        out_ref[m] = jnp.where(live_ref[m] > 0, part, 0.0).astype(bf16)


def input_gradients(live, ranks, second, product):
    micro, rank = ranks.shape[:2]
    rows, width = product.shape
    pieces, _, piece = second.shape
    steps = 2
    return pl.pallas_call(
        functools.partial(gradient_kernel, micro),
        grid=(steps,),
        out_shape=jax.ShapeDtypeStruct((micro, BLOCK_ROWS, width), bf16),
        in_specs=[
            smem(),
            pl.BlockSpec(ranks.shape, lambda i: (0, 0, 0)),
            pl.BlockSpec((pieces // steps, micro * rank, piece), lambda i: (i, 0, 0)),
            pl.BlockSpec((rows, width // steps), lambda i: (0, i)),
        ],
        out_specs=pl.BlockSpec((micro, BLOCK_ROWS, width // steps), lambda i: (0, 0, i)),
        compiler_params=pltpu.CompilerParams(vmem_limit_bytes=WIDE_LIMIT),
        cost_estimate=pl.CostEstimate(
            flops=2 * rows * width * rank, bytes_accessed=6 * rows * width, transcendentals=0
        ),
        name="input_gradients",
    )(live, ranks, second, product)


def layer_kernel(micro, live_ref, ranks_ref, up_ref, *refs):
    out_ref = refs[-1]
    for m in range(micro):
        total = adapter_scale * tn_dot(ranks_ref[m], up_ref[m].astype(bf16))
        for part_ref in refs[:-1]:
            total += part_ref[m * BLOCK_ROWS : (m + 1) * BLOCK_ROWS, :].astype(f32)
        out_ref[m] = jnp.where(live_ref[m] > 0, total, 0.0).astype(bf16)


def layer_outputs(live, ranks, up, parts):
    micro, _, columns = up.shape
    return pl.pallas_call(
        functools.partial(layer_kernel, micro),
        out_shape=jax.ShapeDtypeStruct((micro, BLOCK_ROWS, columns), bf16),
        in_specs=[smem()] + [pl.BlockSpec(memory_space=pltpu.VMEM)] * (2 + len(parts)),
        out_specs=pl.BlockSpec(memory_space=pltpu.VMEM),
        compiler_params=params(),
        name="layer_outputs",
    )(live, ranks, up, *parts)


def rank_kernel(parts_ref, incoming_ref, ranks_ref, pieces_ref):
    micro, rank = parts_ref.shape[2:4]
    total = parts_ref[0].astype(f32)
    for q in range(1, parts_ref.shape[0]):
        total += parts_ref[q].astype(f32)
    ranks_ref[...] = total.astype(bf16)
    half = rank // 2
    for m in range(micro):
        grad = jnp.dot(ranks_ref[0, m], incoming_ref[m], preferred_element_type=f32)
        grad = (grad * (adapter_scale / BLOCK_ROWS)).astype(bf16)
        for p in range(pieces_ref.shape[0]):
            top = (p % 2) * half
            pieces_ref[p, m] = grad[top : top + half]


def ranks_and_pieces(parts, incoming, holders):
    micro, rank = parts.shape[2:4]
    columns = incoming.shape[2]
    return pl.pallas_call(
        rank_kernel,
        out_shape=(
            jax.ShapeDtypeStruct(parts.shape[1:], bf16),
            jax.ShapeDtypeStruct((holders, micro, rank // 2, columns), bf16),
        ),
        in_specs=[pl.BlockSpec(memory_space=pltpu.VMEM)] * 2,
        out_specs=(pl.BlockSpec(memory_space=pltpu.VMEM),) * 2,
        compiler_params=params(),
        name="ranks_and_pieces",
    )(parts, incoming)


def slot_kernel(marks_ref, first_ref, pieces_ref, out_ref):
    holders, micro = pieces_ref.shape[:2]
    out_ref[...] = jnp.zeros_like(out_ref)
    for d in range(holders):
        marks = [marks_ref[d * micro + m] for m in range(micro)]
        for i in range(out_ref.shape[0]):
            hits = [mark == first_ref[0] + i for mark in marks]

            @pl.when(functools.reduce(jnp.logical_or, hits))
            def _():
                partial = None
                for m in range(micro):
                    term = jnp.where(hits[m], pieces_ref[d, m].astype(f32), 0.0)
                    partial = term if partial is None else partial + term
                out_ref[i, 0] += partial
                out_ref[i, 1] += partial * partial


def slot_sums(marks, first_slot, pieces, own_slots):
    return pl.pallas_call(
        slot_kernel,
        out_shape=jax.ShapeDtypeStruct((own_slots, 2) + pieces.shape[2:], f32),
        in_specs=[smem(), smem(), pl.BlockSpec(memory_space=pltpu.VMEM)],
        out_specs=pl.BlockSpec(memory_space=pltpu.VMEM),
        compiler_params=params(),
        name="slot_sums",
    )(marks, first_slot, pieces)


def place_kernel(core_ref, own_ref, other_ref, sum_ref, square_ref):
    half = own_ref.shape[2]
    low = core_ref[0] == 0
    for k in range(own_ref.shape[0]):
        for kind, out_ref in enumerate((sum_ref, square_ref)):
            own, other = own_ref[k, kind], other_ref[k, kind]
            out_ref[k, :half] = jnp.where(low, own, other)
            out_ref[k, half:] = jnp.where(low, other, own)


def placed(core, own, other):
    own_slots, _, half, columns = own.shape
    shape = jax.ShapeDtypeStruct((own_slots, 2 * half, columns), f32)
    return pl.pallas_call(
        place_kernel,
        out_shape=(shape, shape),
        in_specs=[smem()] + [pl.BlockSpec(memory_space=pltpu.VMEM)] * 2,
        out_specs=(pl.BlockSpec(memory_space=pltpu.VMEM),) * 2,
        compiler_params=params(),
        name="placed_sums",
    )(core, own, other)


def shards(
    activations, cotangent, base_weight, adapter_down, adapter_up, slot_language, block_language
):
    holders = lax.axis_size("dp")
    quarters = lax.axis_size("mp")
    own_slots, width, rank = adapter_down.shape[1:]
    columns = adapter_up.shape[3]
    micro = activations.shape[1]
    rows = micro * BLOCK_ROWS
    piece = width // holders
    up_groups = holders // (columns // LANES)
    up_rows = rank // up_groups
    me = lax.axis_index("dp")

    returned = passed_along(cotangent, "section", -1)[0]
    arrived = [passed_along(activations[:, m : m + 1], "section", 1) for m in range(micro)]

    slot_table = slot_language[0]
    langs = block_language[0, :, 0]
    live = (langs < slot_table.shape[0]).astype(jnp.int32)

    weight = jnp.swapaxes(base_weight[0], 0, 1)
    flat_cots = returned.reshape(rows, columns)
    cots = [flat_cots] + [
        lax.ppermute(flat_cots, "mp", [(i, (i + k) % quarters) for i in range(quarters)])
        for k in range(1, quarters)
    ]

    down = jnp.swapaxes(adapter_down[0], 1, 2)
    first = packed(langs[None, :], slot_language, down, adapter_up[0], holders)
    first, weight = lax.optimization_barrier((first, weight))
    gathered = lax.all_gather(weight, "dp", axis=0)
    first = exchanged(first, "dp")

    marked = own_slots * (rank + up_rows)
    slots = first[:, marked : marked + micro, 0].astype(jnp.int32).reshape(-1)
    second = selected(slots, first, micro, own_slots, rank, up_rows)
    second, arrived[0], cots[1] = lax.optimization_barrier((second, arrived[0], cots[1]))
    second = exchanged(second, "dp")
    second, cots = lax.optimization_barrier((second, cots))

    parts, up = rank_parts(second, returned, arrived, rank, quarters)
    parts = exchanged(parts, "mp")
    quarter = lax.axis_index("mp").astype(jnp.int32).reshape(1)
    base_parts, back = weight_products(quarter, arrived, cots, gathered)
    parts, base_parts = lax.optimization_barrier((parts, base_parts))
    ranks, pieces = ranks_and_pieces(parts, returned, holders)
    rank_in, rank_back = ranks[0], ranks[1]

    pieces = exchanged(pieces, "dp")
    base_parts = [base_parts[0]] + [
        lax.ppermute(base_parts[k], "mp", [(i, (i + k) % quarters) for i in range(quarters)])
        for k in range(1, quarters)
    ]
    layer_out = layer_outputs(live, rank_in, up, base_parts)[None]
    input_gradient = input_gradients(live, rank_back, second, back)[None]
    pieces, input_gradient, layer_out = lax.optimization_barrier(
        (pieces, input_gradient, layer_out)
    )
    other = slot_sums(slots, (own_slots * (me ^ 1)).astype(jnp.int32).reshape(1), pieces, own_slots)
    other = lax.ppermute(other, "dp", [(i, i ^ 1) for i in range(holders)])
    own = slot_sums(slots, (own_slots * me).astype(jnp.int32).reshape(1), pieces, own_slots)
    grad_sum, grad_square = placed((me % 2).astype(jnp.int32).reshape(1), own, other)

    return (layer_out, input_gradient, grad_sum[None], grad_square[None])


def solution(mesh):
    in_specs = (
        P("section", None, "dp", "mp"),
        P("section", None, "dp", "mp"),
        P("section", "mp", "dp"),
        P("section", "dp", "mp", None),
        P("section", "dp", None, "mp"),
        P("section", None),
        P("section", None, "dp"),
    )
    out_specs = (
        P("section", None, "dp", "mp"),
        P("section", None, "dp", "mp"),
        P("section", "dp", None, "mp"),
        P("section", "dp", None, "mp"),
    )
    return jax.shard_map(shards, mesh=mesh, in_specs=in_specs, out_specs=out_specs, check_vma=False)
```

```python
import functools

import jax
import jax.numpy as jnp
from jax import lax
from jax.experimental import pallas as pl
from jax.experimental.pallas import tpu as pltpu
from jax.sharding import PartitionSpec as P

BLOCK_ROWS = 128
LANES = 128

adapter_scale = 2.0

bf16, f32 = jnp.bfloat16, jnp.float32
VMEM_LIMIT = 24 * 1024 * 1024
WIDE_LIMIT = 60 * 1024 * 1024
PARTS = 4


def passed_along(array, axis, by):
    devices = lax.axis_size(axis)
    return lax.ppermute(array, axis, [(i, (i + by) % devices) for i in range(devices)])


def exchanged(array, axis):
    return lax.all_to_all(array, axis, split_axis=0, concat_axis=0, tiled=True)


def smem():
    return pl.BlockSpec(memory_space=pltpu.SMEM)


def params():
    return pltpu.CompilerParams(vmem_limit_bytes=VMEM_LIMIT)


def nt_dot(a, b):
    return lax.dot_general(a, b, (((1,), (1,)), ((), ())), preferred_element_type=f32)


def tn_dot(a, b):
    return lax.dot_general(a, b, (((0,), (0,)), ((), ())), preferred_element_type=f32)


def started(source, target, sem):
    copy = pltpu.make_async_copy(source, target, sem)
    copy.start()
    return copy


def pack_kernel(halves, langs_ref, table_ref, down_ref, up_ref, out_ref):
    pieces, payload, piece = out_ref.shape
    own_slots, rank, _ = down_ref.shape
    micro, count = langs_ref.shape[1], table_ref.shape[1]
    group = up_ref.shape[1] * halves // pieces
    low, high = own_slots * rank, own_slots * (rank + group)
    lane = lax.broadcasted_iota(jnp.int32, (1, count), 1)
    row = lax.broadcasted_iota(jnp.int32, (payload - high, piece), 0)
    marks = jnp.zeros((payload - high, piece), f32)
    for m in range(micro):
        match = table_ref[...] == langs_ref[:, m : m + 1]
        slot = jnp.min(jnp.where(match, lane, count), axis=1, keepdims=True).astype(f32)
        marks = jnp.where(row == m, slot, marks)
    marks = marks.astype(bf16)
    ups = [up_ref[k].astype(f32) for k in range(own_slots)]
    for p in range(pieces):
        for k in range(own_slots):
            out_ref[p, k * rank : (k + 1) * rank, :] = down_ref[k, :, p * piece : (p + 1) * piece]
        top, left = (p // halves) * group, (p % halves) * LANES
        out_ref[p, low:high, :] = jnp.concatenate(
            [up[top : top + group, left : left + LANES] for up in ups], axis=0
        ).astype(bf16)
        out_ref[p, high:, :] = marks


def packed(langs, table, down, up, holders):
    own_slots, rank, width = down.shape
    columns = up.shape[2]
    halves = columns // LANES
    payload = own_slots * (rank + rank * halves // holders) + 8
    steps = 1
    return pl.pallas_call(
        functools.partial(pack_kernel, halves),
        grid=(steps,),
        out_shape=jax.ShapeDtypeStruct((holders, payload, width // holders), bf16),
        in_specs=[
            pl.BlockSpec(langs.shape, lambda i: (0, 0)),
            pl.BlockSpec(table.shape, lambda i: (0, 0)),
            pl.BlockSpec((own_slots, rank, width // steps), lambda i: (0, 0, i)),
            pl.BlockSpec((own_slots, rank // steps, columns), lambda i: (0, i, 0)),
        ],
        out_specs=pl.BlockSpec(
            (holders // steps, payload, width // holders), lambda i: (i, 0, 0)
        ),
        compiler_params=pltpu.CompilerParams(vmem_limit_bytes=WIDE_LIMIT),
        name="packed_adapters",
    )(langs, table, down, up)


def weight_kernel(micro, quarters, first_ref, *refs):
    acts, cots = refs[:micro], refs[micro : micro + quarters]
    gathered_ref = refs[micro + quarters]
    outs, back_ref = refs[micro + quarters + 1 : -1], refs[-1]
    holders, _, width = gathered_ref.shape
    group = holders // quarters
    rows = jnp.concatenate([ref[0, 0] for ref in acts], axis=0)
    for k in range(quarters):
        quarter = lax.rem(first_ref[0] + k, quarters)
        weight = gathered_ref[pl.ds(quarter * group, group)].reshape(-1, width)
        outs[k][...] = nt_dot(rows, weight).astype(bf16)
        back = jnp.dot(cots[(quarters - k) % quarters][...], weight, preferred_element_type=f32)
        if k == 0:
            back_ref[...] = back
        else:
            back_ref[...] += back


def weight_products(first, acts, cots, gathered):
    micro, quarters = len(acts), len(cots)
    holders, cols, width = gathered.shape
    rows = micro * BLOCK_ROWS
    group = holders // quarters
    results = pl.pallas_call(
        functools.partial(weight_kernel, micro, quarters),
        out_shape=(jax.ShapeDtypeStruct((rows, group * cols), bf16),) * quarters
        + (jax.ShapeDtypeStruct((rows, width), f32),),
        in_specs=[smem()] + [pl.BlockSpec(memory_space=pltpu.VMEM)] * (micro + quarters + 1),
        out_specs=(pl.BlockSpec(memory_space=pltpu.VMEM),) * (quarters + 1),
        compiler_params=pltpu.CompilerParams(vmem_limit_bytes=VMEM_LIMIT),
        cost_estimate=pl.CostEstimate(
            flops=4 * rows * width * cols * holders,
            bytes_accessed=2 * holders * cols * (width + 2 * rows) + 4 * rows * width,
            transcendentals=0,
        ),
        name="weight_products",
    )(first, *acts, *cots, gathered)
    return list(results[:-1]), results[-1]


def part_kernel(micro, second_ref, returned_ref, *refs):
    acts, parts_ref, up_ref = refs[:micro], refs[micro], refs[micro + 1]
    pieces, _, piece = second_ref.shape
    rank, columns = up_ref.shape[1:]
    halves = columns // LANES
    group = rank * halves // pieces
    for p in range(pieces):
        both = second_ref[p, micro * rank :, :].astype(f32)
        top, left = (p // halves) * group, (p % halves) * LANES
        for m in range(micro):
            up_ref[m, top : top + group, left : left + LANES] = both[m * group : (m + 1) * group]
    for m in range(micro):
        down = jnp.concatenate(
            [second_ref[p, m * rank : (m + 1) * rank, :] for p in range(pieces)], axis=1
        )
        parts = (
            nt_dot(down, acts[m][0, 0]).astype(bf16),
            nt_dot(up_ref[m].astype(bf16), returned_ref[m]).astype(bf16),
        )
        for q in range(parts_ref.shape[0]):
            for kind in range(2):
                parts_ref[q, kind, m] = parts[kind]


def rank_parts(second, returned, acts, rank, quarters):
    micro, _, columns = returned.shape
    return pl.pallas_call(
        functools.partial(part_kernel, micro),
        out_shape=(
            jax.ShapeDtypeStruct((quarters, 2, micro, rank, BLOCK_ROWS), bf16),
            jax.ShapeDtypeStruct((micro, rank, columns), f32),
        ),
        in_specs=[pl.BlockSpec(memory_space=pltpu.VMEM)] * (2 + micro),
        out_specs=(pl.BlockSpec(memory_space=pltpu.VMEM),) * 2,
        compiler_params=params(),
        name="rank_parts",
    )(second, returned, *acts)


def select_kernel(micro, own_slots, rank, slots_ref, first_ref, out, out_ref, sems):
    holders = out_ref.shape[0]
    group = out_ref.shape[1] // micro - rank
    low = own_slots * rank
    chunk = holders // PARTS
    sent = []
    for i in range(PARTS):
        for d in range(i * chunk, (i + 1) * chunk):
            ups = []
            for m in range(micro):
                slot = jnp.minimum(slots_ref[d * micro + m], holders * own_slots - 1)
                owner, k = lax.div(slot, own_slots), lax.rem(slot, own_slots)
                rows = pl.ds(pl.multiple_of(k * rank, rank), rank)
                out_ref[d, m * rank : (m + 1) * rank, :] = first_ref[owner, rows, :]
                held = first_ref[owner, low : low + own_slots * group, :].astype(f32)
                up = held[:group]
                for j in range(1, own_slots):
                    up = jnp.where(k == j, held[j * group : (j + 1) * group], up)
                ups.append(up)
            out_ref[d, micro * rank :, :] = jnp.concatenate(ups, axis=0).astype(bf16)
        some = pl.ds(i * chunk, chunk)
        sent.append(started(out_ref.at[some], out.at[some], sems.at[i]))
    for copy in sent:
        copy.wait()


def selected(slots, first, micro, own_slots, rank, group):
    holders, _, lanes = first.shape
    out = (holders, micro * (rank + group), lanes)
    return pl.pallas_call(
        functools.partial(select_kernel, micro, own_slots, rank),
        out_shape=jax.ShapeDtypeStruct(out, bf16),
        in_specs=[smem(), pl.BlockSpec(memory_space=pltpu.VMEM)],
        out_specs=pl.BlockSpec(memory_space=pl.ANY),
        scratch_shapes=[pltpu.VMEM(out, bf16), pltpu.SemaphoreType.DMA((PARTS,))],
        compiler_params=params(),
        name="selected_pieces",
    )(slots, first)


def gradient_kernel(micro, live_ref, ranks_ref, down_ref, product_ref, out_ref):
    rank = ranks_ref.shape[1]
    pieces = down_ref.shape[0]
    for m in range(micro):
        back = (adapter_scale * ranks_ref[m].astype(f32)).T.astype(bf16)
        down = jnp.concatenate(
            [down_ref[p, m * rank : (m + 1) * rank, :] for p in range(pieces)], axis=1
        )
        lora = jnp.dot(back, down, preferred_element_type=f32).astype(bf16).astype(f32)
        part = product_ref[m * BLOCK_ROWS : (m + 1) * BLOCK_ROWS] + lora
        out_ref[m] = jnp.where(live_ref[m] > 0, part, 0.0).astype(bf16)


def input_gradients(live, ranks, second, product):
    micro, rank = ranks.shape[:2]
    rows, width = product.shape
    pieces, _, piece = second.shape
    steps = 2
    return pl.pallas_call(
        functools.partial(gradient_kernel, micro),
        grid=(steps,),
        out_shape=jax.ShapeDtypeStruct((micro, BLOCK_ROWS, width), bf16),
        in_specs=[
            smem(),
            pl.BlockSpec(ranks.shape, lambda i: (0, 0, 0)),
            pl.BlockSpec((pieces // steps, micro * rank, piece), lambda i: (i, 0, 0)),
            pl.BlockSpec((rows, width // steps), lambda i: (0, i)),
        ],
        out_specs=pl.BlockSpec((micro, BLOCK_ROWS, width // steps), lambda i: (0, 0, i)),
        compiler_params=pltpu.CompilerParams(vmem_limit_bytes=WIDE_LIMIT),
        cost_estimate=pl.CostEstimate(
            flops=2 * rows * width * rank, bytes_accessed=6 * rows * width, transcendentals=0
        ),
        name="input_gradients",
    )(live, ranks, second, product)


def layer_kernel(micro, live_ref, ranks_ref, up_ref, *refs):
    out_ref = refs[-1]
    for m in range(micro):
        total = adapter_scale * tn_dot(ranks_ref[m], up_ref[m].astype(bf16))
        for part_ref in refs[:-1]:
            total += part_ref[m * BLOCK_ROWS : (m + 1) * BLOCK_ROWS, :].astype(f32)
        out_ref[m] = jnp.where(live_ref[m] > 0, total, 0.0).astype(bf16)


def layer_outputs(live, ranks, up, parts):
    micro, _, columns = up.shape
    return pl.pallas_call(
        functools.partial(layer_kernel, micro),
        out_shape=jax.ShapeDtypeStruct((micro, BLOCK_ROWS, columns), bf16),
        in_specs=[smem()] + [pl.BlockSpec(memory_space=pltpu.VMEM)] * (2 + len(parts)),
        out_specs=pl.BlockSpec(memory_space=pltpu.VMEM),
        compiler_params=params(),
        name="layer_outputs",
    )(live, ranks, up, *parts)


def rank_kernel(parts_ref, incoming_ref, ranks_ref, pieces_ref):
    micro, rank = parts_ref.shape[2:4]
    total = parts_ref[0].astype(f32)
    for q in range(1, parts_ref.shape[0]):
        total += parts_ref[q].astype(f32)
    ranks_ref[...] = total.astype(bf16)
    half = rank // 2
    for m in range(micro):
        grad = jnp.dot(ranks_ref[0, m], incoming_ref[m], preferred_element_type=f32)
        grad = (grad * (adapter_scale / BLOCK_ROWS)).astype(bf16)
        for p in range(pieces_ref.shape[0]):
            top = (p % 2) * half
            pieces_ref[p, m] = grad[top : top + half]


def ranks_and_pieces(parts, incoming, holders):
    micro, rank = parts.shape[2:4]
    columns = incoming.shape[2]
    return pl.pallas_call(
        rank_kernel,
        out_shape=(
            jax.ShapeDtypeStruct(parts.shape[1:], bf16),
            jax.ShapeDtypeStruct((holders, micro, rank // 2, columns), bf16),
        ),
        in_specs=[pl.BlockSpec(memory_space=pltpu.VMEM)] * 2,
        out_specs=(pl.BlockSpec(memory_space=pltpu.VMEM),) * 2,
        compiler_params=params(),
        name="ranks_and_pieces",
    )(parts, incoming)


def slot_kernel(marks_ref, first_ref, pieces_ref, out_ref):
    holders, micro = pieces_ref.shape[:2]
    out_ref[...] = jnp.zeros_like(out_ref)
    for d in range(holders):
        marks = [marks_ref[d * micro + m] for m in range(micro)]
        for i in range(out_ref.shape[0]):
            hits = [mark == first_ref[0] + i for mark in marks]

            @pl.when(functools.reduce(jnp.logical_or, hits))
            def _():
                partial = None
                for m in range(micro):
                    term = jnp.where(hits[m], pieces_ref[d, m].astype(f32), 0.0)
                    partial = term if partial is None else partial + term
                out_ref[i, 0] += partial
                out_ref[i, 1] += partial * partial


def slot_sums(marks, first_slot, pieces, own_slots):
    return pl.pallas_call(
        slot_kernel,
        out_shape=jax.ShapeDtypeStruct((own_slots, 2) + pieces.shape[2:], f32),
        in_specs=[smem(), smem(), pl.BlockSpec(memory_space=pltpu.VMEM)],
        out_specs=pl.BlockSpec(memory_space=pltpu.VMEM),
        compiler_params=params(),
        name="slot_sums",
    )(marks, first_slot, pieces)


def place_kernel(core_ref, own_ref, other_ref, sum_ref, square_ref):
    half = own_ref.shape[2]
    low = core_ref[0] == 0
    for k in range(own_ref.shape[0]):
        for kind, out_ref in enumerate((sum_ref, square_ref)):
            own, other = own_ref[k, kind], other_ref[k, kind]
            out_ref[k, :half] = jnp.where(low, own, other)
            out_ref[k, half:] = jnp.where(low, other, own)


def placed(core, own, other):
    own_slots, _, half, columns = own.shape
    shape = jax.ShapeDtypeStruct((own_slots, 2 * half, columns), f32)
    return pl.pallas_call(
        place_kernel,
        out_shape=(shape, shape),
        in_specs=[smem()] + [pl.BlockSpec(memory_space=pltpu.VMEM)] * 2,
        out_specs=(pl.BlockSpec(memory_space=pltpu.VMEM),) * 2,
        compiler_params=params(),
        name="placed_sums",
    )(core, own, other)


def shards(
    activations, cotangent, base_weight, adapter_down, adapter_up, slot_language, block_language
):
    holders = lax.axis_size("dp")
    quarters = lax.axis_size("mp")
    own_slots, width, rank = adapter_down.shape[1:]
    columns = adapter_up.shape[3]
    micro = activations.shape[1]
    rows = micro * BLOCK_ROWS
    piece = width // holders
    up_groups = holders // (columns // LANES)
    up_rows = rank // up_groups
    me = lax.axis_index("dp")

    returned = passed_along(cotangent, "section", -1)[0]
    arrived = [passed_along(activations[:, m : m + 1], "section", 1) for m in range(micro)]

    slot_table = slot_language[0]
    langs = block_language[0, :, 0]
    live = (langs < slot_table.shape[0]).astype(jnp.int32)

    weight = jnp.swapaxes(base_weight[0], 0, 1)
    flat_cots = returned.reshape(rows, columns)
    cots = [flat_cots] + [
        lax.ppermute(flat_cots, "mp", [(i, (i + k) % quarters) for i in range(quarters)])
        for k in range(1, quarters)
    ]

    down = jnp.swapaxes(adapter_down[0], 1, 2)
    first = packed(langs[None, :], slot_language, down, adapter_up[0], holders)
    first, weight = lax.optimization_barrier((first, weight))
    gathered = lax.all_gather(weight, "dp", axis=0)
    first = exchanged(first, "dp")

    marked = own_slots * (rank + up_rows)
    slots = first[:, marked : marked + micro, 0].astype(jnp.int32).reshape(-1)
    second = selected(slots, first, micro, own_slots, rank, up_rows)
    second, arrived[0], cots[1] = lax.optimization_barrier((second, arrived[0], cots[1]))
    second = exchanged(second, "dp")
    second, cots = lax.optimization_barrier((second, cots))

    parts, up = rank_parts(second, returned, arrived, rank, quarters)
    parts = exchanged(parts, "mp")
    quarter = lax.axis_index("mp").astype(jnp.int32).reshape(1)
    base_parts, back = weight_products(quarter, arrived, cots, gathered)
    parts, base_parts = lax.optimization_barrier((parts, base_parts))
    ranks, pieces = ranks_and_pieces(parts, returned, holders)
    rank_in, rank_back = ranks[0], ranks[1]

    pieces = exchanged(pieces, "dp")
    base_parts = [base_parts[0]] + [
        lax.ppermute(base_parts[k], "mp", [(i, (i + k) % quarters) for i in range(quarters)])
        for k in range(1, quarters)
    ]
    layer_out = layer_outputs(live, rank_in, up, base_parts)[None]
    input_gradient = input_gradients(live, rank_back, second, back)[None]
    pieces, input_gradient, layer_out = lax.optimization_barrier(
        (pieces, input_gradient, layer_out)
    )
    other = slot_sums(slots, (own_slots * (me ^ 1)).astype(jnp.int32).reshape(1), pieces, own_slots)
    other = lax.ppermute(other, "dp", [(i, i ^ 1) for i in range(holders)])
    own = slot_sums(slots, (own_slots * me).astype(jnp.int32).reshape(1), pieces, own_slots)
    grad_sum, grad_square = placed((me % 2).astype(jnp.int32).reshape(1), own, other)

    return (layer_out, input_gradient, grad_sum[None], grad_square[None])


def solution(mesh):
    in_specs = (
        P("section", None, "dp", "mp"),
        P("section", None, "dp", "mp"),
        P("section", "mp", "dp"),
        P("section", "dp", "mp", None),
        P("section", "dp", None, "mp"),
        P("section", None),
        P("section", None, "dp"),
    )
    out_specs = (
        P("section", None, "dp", "mp"),
        P("section", None, "dp", "mp"),
        P("section", "dp", None, "mp"),
        P("section", "dp", None, "mp"),
    )
    return jax.shard_map(shards, mesh=mesh, in_specs=in_specs, out_specs=out_specs, check_vma=False)
```

```python
import functools

import jax
import jax.numpy as jnp
from jax import lax
from jax.experimental import pallas as pl
from jax.experimental.pallas import tpu as pltpu
from jax.sharding import PartitionSpec as P

BLOCK_ROWS = 128
LANES = 128

adapter_scale = 2.0

bf16, f32 = jnp.bfloat16, jnp.float32
VMEM_LIMIT = 24 * 1024 * 1024
WIDE_LIMIT = 60 * 1024 * 1024
PARTS = 4


def passed_along(array, axis, by):
    devices = lax.axis_size(axis)
    return lax.ppermute(array, axis, [(i, (i + by) % devices) for i in range(devices)])


def exchanged(array, axis):
    return lax.all_to_all(array, axis, split_axis=0, concat_axis=0, tiled=True)


def smem():
    return pl.BlockSpec(memory_space=pltpu.SMEM)


def params():
    return pltpu.CompilerParams(vmem_limit_bytes=VMEM_LIMIT)


def nt_dot(a, b):
    return lax.dot_general(a, b, (((1,), (1,)), ((), ())), preferred_element_type=f32)


def tn_dot(a, b):
    return lax.dot_general(a, b, (((0,), (0,)), ((), ())), preferred_element_type=f32)


def started(source, target, sem):
    copy = pltpu.make_async_copy(source, target, sem)
    copy.start()
    return copy


def pack_kernel(halves, langs_ref, table_ref, down_ref, up_ref, out_ref):
    pieces, payload, piece = out_ref.shape
    own_slots, rank, _ = down_ref.shape
    micro, count = langs_ref.shape[1], table_ref.shape[1]
    group = up_ref.shape[1] * halves // pieces
    low, high = own_slots * rank, own_slots * (rank + group)
    lane = lax.broadcasted_iota(jnp.int32, (1, count), 1)
    row = lax.broadcasted_iota(jnp.int32, (payload - high, piece), 0)
    marks = jnp.zeros((payload - high, piece), f32)
    for m in range(micro):
        match = table_ref[...] == langs_ref[:, m : m + 1]
        slot = jnp.min(jnp.where(match, lane, count), axis=1, keepdims=True).astype(f32)
        marks = jnp.where(row == m, slot, marks)
    marks = marks.astype(bf16)
    ups = [up_ref[k].astype(f32) for k in range(own_slots)]
    for p in range(pieces):
        for k in range(own_slots):
            out_ref[p, k * rank : (k + 1) * rank, :] = down_ref[k, :, p * piece : (p + 1) * piece]
        top, left = (p // halves) * group, (p % halves) * LANES
        out_ref[p, low:high, :] = jnp.concatenate(
            [up[top : top + group, left : left + LANES] for up in ups], axis=0
        ).astype(bf16)
        out_ref[p, high:, :] = marks


def packed(langs, table, down, up, holders):
    own_slots, rank, width = down.shape
    columns = up.shape[2]
    halves = columns // LANES
    payload = own_slots * (rank + rank * halves // holders) + 8
    steps = 1
    return pl.pallas_call(
        functools.partial(pack_kernel, halves),
        grid=(steps,),
        out_shape=jax.ShapeDtypeStruct((holders, payload, width // holders), bf16),
        in_specs=[
            pl.BlockSpec(langs.shape, lambda i: (0, 0)),
            pl.BlockSpec(table.shape, lambda i: (0, 0)),
            pl.BlockSpec((own_slots, rank, width // steps), lambda i: (0, 0, i)),
            pl.BlockSpec((own_slots, rank // steps, columns), lambda i: (0, i, 0)),
        ],
        out_specs=pl.BlockSpec(
            (holders // steps, payload, width // holders), lambda i: (i, 0, 0)
        ),
        compiler_params=pltpu.CompilerParams(vmem_limit_bytes=WIDE_LIMIT),
        name="packed_adapters",
    )(langs, table, down, up)


def weight_kernel(micro, quarters, first_ref, *refs):
    acts, cots = refs[:micro], refs[micro : micro + quarters]
    gathered_ref = refs[micro + quarters]
    outs, back_out = refs[micro + quarters + 1 : -3], refs[-3]
    back_ref, sem = refs[-2], refs[-1]
    holders, _, width = gathered_ref.shape
    group = holders // quarters

    def weight(k):
        quarter = lax.rem(first_ref[0] + k, quarters)
        return gathered_ref[pl.ds(quarter * group, group)].reshape(-1, width)

    for k in range(quarters):
        part = cots[(quarters - k) % quarters][...]
        back = jnp.dot(part, weight(k), preferred_element_type=f32)
        if k == 0:
            back_ref[...] = back
        else:
            back_ref[...] += back
    copy = started(back_ref, back_out, sem)
    rows = jnp.concatenate([ref[0, 0] for ref in acts], axis=0)
    for k in range(quarters):
        outs[k][...] = nt_dot(rows, weight(k)).astype(bf16)
    copy.wait()


def weight_products(first, acts, cots, gathered):
    micro, quarters = len(acts), len(cots)
    holders, cols, width = gathered.shape
    rows = micro * BLOCK_ROWS
    group = holders // quarters
    results = pl.pallas_call(
        functools.partial(weight_kernel, micro, quarters),
        out_shape=(jax.ShapeDtypeStruct((rows, group * cols), bf16),) * quarters
        + (jax.ShapeDtypeStruct((rows, width), f32),),
        in_specs=[smem()] + [pl.BlockSpec(memory_space=pltpu.VMEM)] * (micro + quarters + 1),
        out_specs=(pl.BlockSpec(memory_space=pltpu.VMEM),) * quarters
        + (pl.BlockSpec(memory_space=pl.ANY),),
        scratch_shapes=[pltpu.VMEM((rows, width), f32), pltpu.SemaphoreType.DMA],
        compiler_params=pltpu.CompilerParams(vmem_limit_bytes=VMEM_LIMIT),
        cost_estimate=pl.CostEstimate(
            flops=4 * rows * width * cols * holders,
            bytes_accessed=2 * holders * cols * (width + 2 * rows) + 4 * rows * width,
            transcendentals=0,
        ),
        name="weight_products",
    )(first, *acts, *cots, gathered)
    return list(results[:-1]), results[-1]


def part_kernel(micro, second_ref, returned_ref, *refs):
    acts, parts_ref, up_ref = refs[:micro], refs[micro], refs[micro + 1]
    pieces, _, piece = second_ref.shape
    rank, columns = up_ref.shape[1:]
    halves = columns // LANES
    group = rank * halves // pieces
    for p in range(pieces):
        both = second_ref[p, micro * rank :, :].astype(f32)
        top, left = (p // halves) * group, (p % halves) * LANES
        for m in range(micro):
            up_ref[m, top : top + group, left : left + LANES] = both[m * group : (m + 1) * group]
    for m in range(micro):
        down = jnp.concatenate(
            [second_ref[p, m * rank : (m + 1) * rank, :] for p in range(pieces)], axis=1
        )
        parts = (
            nt_dot(down, acts[m][0, 0]).astype(bf16),
            nt_dot(up_ref[m].astype(bf16), returned_ref[m]).astype(bf16),
        )
        for q in range(parts_ref.shape[0]):
            for kind in range(2):
                parts_ref[q, kind, m] = parts[kind]


def rank_parts(second, returned, acts, rank, quarters):
    micro, _, columns = returned.shape
    return pl.pallas_call(
        functools.partial(part_kernel, micro),
        out_shape=(
            jax.ShapeDtypeStruct((quarters, 2, micro, rank, BLOCK_ROWS), bf16),
            jax.ShapeDtypeStruct((micro, rank, columns), f32),
        ),
        in_specs=[pl.BlockSpec(memory_space=pltpu.VMEM)] * (2 + micro),
        out_specs=(pl.BlockSpec(memory_space=pltpu.VMEM),) * 2,
        compiler_params=params(),
        name="rank_parts",
    )(second, returned, *acts)


def select_kernel(micro, own_slots, rank, slots_ref, first_ref, out, out_ref, sems):
    holders = out_ref.shape[0]
    group = out_ref.shape[1] // micro - rank
    low = own_slots * rank
    chunk = holders // PARTS
    sent = []
    for i in range(PARTS):
        for d in range(i * chunk, (i + 1) * chunk):
            ups = []
            for m in range(micro):
                slot = jnp.minimum(slots_ref[d * micro + m], holders * own_slots - 1)
                owner, k = lax.div(slot, own_slots), lax.rem(slot, own_slots)
                rows = pl.ds(pl.multiple_of(k * rank, rank), rank)
                out_ref[d, m * rank : (m + 1) * rank, :] = first_ref[owner, rows, :]
                held = first_ref[owner, low : low + own_slots * group, :].astype(f32)
                up = held[:group]
                for j in range(1, own_slots):
                    up = jnp.where(k == j, held[j * group : (j + 1) * group], up)
                ups.append(up)
            out_ref[d, micro * rank :, :] = jnp.concatenate(ups, axis=0).astype(bf16)
        some = pl.ds(i * chunk, chunk)
        sent.append(started(out_ref.at[some], out.at[some], sems.at[i]))
    for copy in sent:
        copy.wait()


def selected(slots, first, micro, own_slots, rank, group):
    holders, _, lanes = first.shape
    out = (holders, micro * (rank + group), lanes)
    return pl.pallas_call(
        functools.partial(select_kernel, micro, own_slots, rank),
        out_shape=jax.ShapeDtypeStruct(out, bf16),
        in_specs=[smem(), pl.BlockSpec(memory_space=pltpu.VMEM)],
        out_specs=pl.BlockSpec(memory_space=pl.ANY),
        scratch_shapes=[pltpu.VMEM(out, bf16), pltpu.SemaphoreType.DMA((PARTS,))],
        compiler_params=params(),
        name="selected_pieces",
    )(slots, first)


def gradient_kernel(micro, live_ref, ranks_ref, down_ref, product_ref, out_ref):
    rank = ranks_ref.shape[1]
    pieces = down_ref.shape[0]
    for m in range(micro):
        back = (adapter_scale * ranks_ref[m].astype(f32)).T.astype(bf16)
        down = jnp.concatenate(
            [down_ref[p, m * rank : (m + 1) * rank, :] for p in range(pieces)], axis=1
        )
        lora = jnp.dot(back, down, preferred_element_type=f32).astype(bf16).astype(f32)
        part = product_ref[m * BLOCK_ROWS : (m + 1) * BLOCK_ROWS] + lora
        out_ref[m] = jnp.where(live_ref[m] > 0, part, 0.0).astype(bf16)


def input_gradients(live, ranks, second, product):
    micro, rank = ranks.shape[:2]
    rows, width = product.shape
    pieces, _, piece = second.shape
    steps = 2
    return pl.pallas_call(
        functools.partial(gradient_kernel, micro),
        grid=(steps,),
        out_shape=jax.ShapeDtypeStruct((micro, BLOCK_ROWS, width), bf16),
        in_specs=[
            smem(),
            pl.BlockSpec(ranks.shape, lambda i: (0, 0, 0)),
            pl.BlockSpec((pieces // steps, micro * rank, piece), lambda i: (i, 0, 0)),
            pl.BlockSpec((rows, width // steps), lambda i: (0, i)),
        ],
        out_specs=pl.BlockSpec((micro, BLOCK_ROWS, width // steps), lambda i: (0, 0, i)),
        compiler_params=pltpu.CompilerParams(vmem_limit_bytes=WIDE_LIMIT),
        cost_estimate=pl.CostEstimate(
            flops=2 * rows * width * rank, bytes_accessed=6 * rows * width, transcendentals=0
        ),
        name="input_gradients",
    )(live, ranks, second, product)


def layer_kernel(micro, live_ref, ranks_ref, up_ref, *refs):
    out_ref = refs[-1]
    for m in range(micro):
        total = adapter_scale * tn_dot(ranks_ref[m], up_ref[m].astype(bf16))
        for part_ref in refs[:-1]:
            total += part_ref[m * BLOCK_ROWS : (m + 1) * BLOCK_ROWS, :].astype(f32)
        out_ref[m] = jnp.where(live_ref[m] > 0, total, 0.0).astype(bf16)


def layer_outputs(live, ranks, up, parts):
    micro, _, columns = up.shape
    return pl.pallas_call(
        functools.partial(layer_kernel, micro),
        out_shape=jax.ShapeDtypeStruct((micro, BLOCK_ROWS, columns), bf16),
        in_specs=[smem()] + [pl.BlockSpec(memory_space=pltpu.VMEM)] * (2 + len(parts)),
        out_specs=pl.BlockSpec(memory_space=pltpu.VMEM),
        compiler_params=params(),
        name="layer_outputs",
    )(live, ranks, up, *parts)


def rank_kernel(parts_ref, incoming_ref, ranks_ref, pieces_ref):
    micro, rank = parts_ref.shape[2:4]
    total = parts_ref[0].astype(f32)
    for q in range(1, parts_ref.shape[0]):
        total += parts_ref[q].astype(f32)
    ranks_ref[...] = total.astype(bf16)
    half = rank // 2
    for m in range(micro):
        grad = jnp.dot(ranks_ref[0, m], incoming_ref[m], preferred_element_type=f32)
        grad = (grad * (adapter_scale / BLOCK_ROWS)).astype(bf16)
        for p in range(pieces_ref.shape[0]):
            top = (p % 2) * half
            pieces_ref[p, m] = grad[top : top + half]


def ranks_and_pieces(parts, incoming, holders):
    micro, rank = parts.shape[2:4]
    columns = incoming.shape[2]
    return pl.pallas_call(
        rank_kernel,
        out_shape=(
            jax.ShapeDtypeStruct(parts.shape[1:], bf16),
            jax.ShapeDtypeStruct((holders, micro, rank // 2, columns), bf16),
        ),
        in_specs=[pl.BlockSpec(memory_space=pltpu.VMEM)] * 2,
        out_specs=(pl.BlockSpec(memory_space=pltpu.VMEM),) * 2,
        compiler_params=params(),
        name="ranks_and_pieces",
    )(parts, incoming)


def slot_kernel(marks_ref, first_ref, pieces_ref, out_ref):
    holders, micro = pieces_ref.shape[:2]
    out_ref[...] = jnp.zeros_like(out_ref)
    for d in range(holders):
        marks = [marks_ref[d * micro + m] for m in range(micro)]
        for i in range(out_ref.shape[0]):
            hits = [mark == first_ref[0] + i for mark in marks]

            @pl.when(functools.reduce(jnp.logical_or, hits))
            def _():
                partial = None
                for m in range(micro):
                    term = jnp.where(hits[m], pieces_ref[d, m].astype(f32), 0.0)
                    partial = term if partial is None else partial + term
                out_ref[i, 0] += partial
                out_ref[i, 1] += partial * partial


def slot_sums(marks, first_slot, pieces, own_slots):
    return pl.pallas_call(
        slot_kernel,
        out_shape=jax.ShapeDtypeStruct((own_slots, 2) + pieces.shape[2:], f32),
        in_specs=[smem(), smem(), pl.BlockSpec(memory_space=pltpu.VMEM)],
        out_specs=pl.BlockSpec(memory_space=pltpu.VMEM),
        compiler_params=params(),
        name="slot_sums",
    )(marks, first_slot, pieces)


def place_kernel(core_ref, own_ref, other_ref, sum_ref, square_ref):
    half = own_ref.shape[2]
    low = core_ref[0] == 0
    for k in range(own_ref.shape[0]):
        for kind, out_ref in enumerate((sum_ref, square_ref)):
            own, other = own_ref[k, kind], other_ref[k, kind]
            out_ref[k, :half] = jnp.where(low, own, other)
            out_ref[k, half:] = jnp.where(low, other, own)


def placed(core, own, other):
    own_slots, _, half, columns = own.shape
    shape = jax.ShapeDtypeStruct((own_slots, 2 * half, columns), f32)
    return pl.pallas_call(
        place_kernel,
        out_shape=(shape, shape),
        in_specs=[smem()] + [pl.BlockSpec(memory_space=pltpu.VMEM)] * 2,
        out_specs=(pl.BlockSpec(memory_space=pltpu.VMEM),) * 2,
        compiler_params=params(),
        name="placed_sums",
    )(core, own, other)


def shards(
    activations, cotangent, base_weight, adapter_down, adapter_up, slot_language, block_language
):
    holders = lax.axis_size("dp")
    quarters = lax.axis_size("mp")
    own_slots, width, rank = adapter_down.shape[1:]
    columns = adapter_up.shape[3]
    micro = activations.shape[1]
    rows = micro * BLOCK_ROWS
    piece = width // holders
    up_groups = holders // (columns // LANES)
    up_rows = rank // up_groups
    me = lax.axis_index("dp")

    returned = passed_along(cotangent, "section", -1)[0]
    arrived = [passed_along(activations[:, m : m + 1], "section", 1) for m in range(micro)]

    slot_table = slot_language[0]
    langs = block_language[0, :, 0]
    live = (langs < slot_table.shape[0]).astype(jnp.int32)

    weight = jnp.swapaxes(base_weight[0], 0, 1)
    flat_cots = returned.reshape(rows, columns)
    cots = [flat_cots] + [
        lax.ppermute(flat_cots, "mp", [(i, (i + k) % quarters) for i in range(quarters)])
        for k in range(1, quarters)
    ]

    down = jnp.swapaxes(adapter_down[0], 1, 2)
    first = packed(langs[None, :], slot_language, down, adapter_up[0], holders)
    first, weight = lax.optimization_barrier((first, weight))
    gathered = lax.all_gather(weight, "dp", axis=0)
    first = exchanged(first, "dp")

    marked = own_slots * (rank + up_rows)
    slots = first[:, marked : marked + micro, 0].astype(jnp.int32).reshape(-1)
    second = selected(slots, first, micro, own_slots, rank, up_rows)
    second, arrived[0], cots[1] = lax.optimization_barrier((second, arrived[0], cots[1]))
    second = exchanged(second, "dp")
    second, cots = lax.optimization_barrier((second, cots))

    parts, up = rank_parts(second, returned, arrived, rank, quarters)
    parts = exchanged(parts, "mp")
    quarter = lax.axis_index("mp").astype(jnp.int32).reshape(1)
    base_parts, back = weight_products(quarter, arrived, cots, gathered)
    parts, base_parts = lax.optimization_barrier((parts, base_parts))
    ranks, pieces = ranks_and_pieces(parts, returned, holders)
    rank_in, rank_back = ranks[0], ranks[1]

    pieces = exchanged(pieces, "dp")
    base_parts = [base_parts[0]] + [
        lax.ppermute(base_parts[k], "mp", [(i, (i + k) % quarters) for i in range(quarters)])
        for k in range(1, quarters)
    ]
    layer_out = layer_outputs(live, rank_in, up, base_parts)[None]
    input_gradient = input_gradients(live, rank_back, second, back)[None]
    pieces, input_gradient, layer_out = lax.optimization_barrier(
        (pieces, input_gradient, layer_out)
    )
    other = slot_sums(slots, (own_slots * (me ^ 1)).astype(jnp.int32).reshape(1), pieces, own_slots)
    other = lax.ppermute(other, "dp", [(i, i ^ 1) for i in range(holders)])
    own = slot_sums(slots, (own_slots * me).astype(jnp.int32).reshape(1), pieces, own_slots)
    grad_sum, grad_square = placed((me % 2).astype(jnp.int32).reshape(1), own, other)

    return (layer_out, input_gradient, grad_sum[None], grad_square[None])


def solution(mesh):
    in_specs = (
        P("section", None, "dp", "mp"),
        P("section", None, "dp", "mp"),
        P("section", "mp", "dp"),
        P("section", "dp", "mp", None),
        P("section", "dp", None, "mp"),
        P("section", None),
        P("section", None, "dp"),
    )
    out_specs = (
        P("section", None, "dp", "mp"),
        P("section", None, "dp", "mp"),
        P("section", "dp", None, "mp"),
        P("section", "dp", None, "mp"),
    )
    return jax.shard_map(shards, mesh=mesh, in_specs=in_specs, out_specs=out_specs, check_vma=False)
```

```python
import functools

import jax
import jax.numpy as jnp
from jax import lax
from jax.experimental import pallas as pl
from jax.experimental.pallas import tpu as pltpu
from jax.sharding import PartitionSpec as P

BLOCK_ROWS = 128
LANES = 128

adapter_scale = 2.0

bf16, f32 = jnp.bfloat16, jnp.float32
VMEM_LIMIT = 24 * 1024 * 1024
WIDE_LIMIT = 60 * 1024 * 1024
PARTS = 4


def passed_along(array, axis, by):
    devices = lax.axis_size(axis)
    return lax.ppermute(array, axis, [(i, (i + by) % devices) for i in range(devices)])


def exchanged(array, axis):
    return lax.all_to_all(array, axis, split_axis=0, concat_axis=0, tiled=True)


def smem():
    return pl.BlockSpec(memory_space=pltpu.SMEM)


def params():
    return pltpu.CompilerParams(vmem_limit_bytes=VMEM_LIMIT)


def nt_dot(a, b):
    return lax.dot_general(a, b, (((1,), (1,)), ((), ())), preferred_element_type=f32)


def tn_dot(a, b):
    return lax.dot_general(a, b, (((0,), (0,)), ((), ())), preferred_element_type=f32)


def started(source, target, sem):
    copy = pltpu.make_async_copy(source, target, sem)
    copy.start()
    return copy


def pack_kernel(halves, langs_ref, table_ref, down_ref, up_ref, out_ref):
    pieces, payload, piece = out_ref.shape
    own_slots, rank, _ = down_ref.shape
    micro, count = langs_ref.shape[1], table_ref.shape[1]
    group = up_ref.shape[1] * halves // pieces
    low, high = own_slots * rank, own_slots * (rank + group)
    lane = lax.broadcasted_iota(jnp.int32, (1, count), 1)
    row = lax.broadcasted_iota(jnp.int32, (payload - high, piece), 0)
    marks = jnp.zeros((payload - high, piece), f32)
    for m in range(micro):
        match = table_ref[...] == langs_ref[:, m : m + 1]
        slot = jnp.min(jnp.where(match, lane, count), axis=1, keepdims=True).astype(f32)
        marks = jnp.where(row == m, slot, marks)
    marks = marks.astype(bf16)
    ups = [up_ref[k].astype(f32) for k in range(own_slots)]
    for p in range(pieces):
        for k in range(own_slots):
            out_ref[p, k * rank : (k + 1) * rank, :] = down_ref[k, :, p * piece : (p + 1) * piece]
        top, left = (p // halves) * group, (p % halves) * LANES
        out_ref[p, low:high, :] = jnp.concatenate(
            [up[top : top + group, left : left + LANES] for up in ups], axis=0
        ).astype(bf16)
        out_ref[p, high:, :] = marks


def packed(langs, table, down, up, holders):
    own_slots, rank, width = down.shape
    columns = up.shape[2]
    halves = columns // LANES
    payload = own_slots * (rank + rank * halves // holders) + 8
    steps = 1
    return pl.pallas_call(
        functools.partial(pack_kernel, halves),
        grid=(steps,),
        out_shape=jax.ShapeDtypeStruct((holders, payload, width // holders), bf16),
        in_specs=[
            pl.BlockSpec(langs.shape, lambda i: (0, 0)),
            pl.BlockSpec(table.shape, lambda i: (0, 0)),
            pl.BlockSpec((own_slots, rank, width // steps), lambda i: (0, 0, i)),
            pl.BlockSpec((own_slots, rank // steps, columns), lambda i: (0, i, 0)),
        ],
        out_specs=pl.BlockSpec(
            (holders // steps, payload, width // holders), lambda i: (i, 0, 0)
        ),
        compiler_params=pltpu.CompilerParams(vmem_limit_bytes=WIDE_LIMIT),
        name="packed_adapters",
    )(langs, table, down, up)


def weight_kernel(micro, quarters, first_ref, *refs):
    acts, cots = refs[:micro], refs[micro : micro + quarters]
    gathered_ref = refs[micro + quarters]
    outs, back_out = refs[micro + quarters + 1 : -3], refs[-3]
    back_ref, sem = refs[-2], refs[-1]
    holders, _, width = gathered_ref.shape
    group = holders // quarters

    def weight(k):
        quarter = lax.rem(first_ref[0] + k, quarters)
        return gathered_ref[pl.ds(quarter * group, group)].reshape(-1, width)

    for k in range(quarters):
        part = cots[(quarters - k) % quarters][...]
        back = jnp.dot(part, weight(k), preferred_element_type=f32)
        if k == 0:
            back_ref[...] = back
        else:
            back_ref[...] += back
    copy = started(back_ref, back_out, sem)
    rows = jnp.concatenate([ref[0, 0] for ref in acts], axis=0)
    for k in range(quarters):
        outs[k][...] = nt_dot(rows, weight(k)).astype(bf16)
    copy.wait()


def weight_products(first, acts, cots, gathered):
    micro, quarters = len(acts), len(cots)
    holders, cols, width = gathered.shape
    rows = micro * BLOCK_ROWS
    group = holders // quarters
    results = pl.pallas_call(
        functools.partial(weight_kernel, micro, quarters),
        out_shape=(jax.ShapeDtypeStruct((rows, group * cols), bf16),) * quarters
        + (jax.ShapeDtypeStruct((rows, width), f32),),
        in_specs=[smem()] + [pl.BlockSpec(memory_space=pltpu.VMEM)] * (micro + quarters + 1),
        out_specs=(pl.BlockSpec(memory_space=pltpu.VMEM),) * quarters
        + (pl.BlockSpec(memory_space=pl.ANY),),
        scratch_shapes=[pltpu.VMEM((rows, width), f32), pltpu.SemaphoreType.DMA],
        compiler_params=pltpu.CompilerParams(vmem_limit_bytes=VMEM_LIMIT),
        cost_estimate=pl.CostEstimate(
            flops=4 * rows * width * cols * holders,
            bytes_accessed=2 * holders * cols * (width + 2 * rows) + 4 * rows * width,
            transcendentals=0,
        ),
        name="weight_products",
    )(first, *acts, *cots, gathered)
    return list(results[:-1]), results[-1]


def part_kernel(micro, second_ref, returned_ref, *refs):
    acts, parts_ref, up_ref = refs[:micro], refs[micro], refs[micro + 1]
    pieces, _, piece = second_ref.shape
    rank, columns = up_ref.shape[1:]
    halves = columns // LANES
    group = rank * halves // pieces
    for p in range(pieces):
        both = second_ref[p, micro * rank :, :].astype(f32)
        top, left = (p // halves) * group, (p % halves) * LANES
        for m in range(micro):
            up_ref[m, top : top + group, left : left + LANES] = both[m * group : (m + 1) * group]
    for m in range(micro):
        down = jnp.concatenate(
            [second_ref[p, m * rank : (m + 1) * rank, :] for p in range(pieces)], axis=1
        )
        parts = (
            nt_dot(down, acts[m][0, 0]).astype(bf16),
            nt_dot(up_ref[m].astype(bf16), returned_ref[m]).astype(bf16),
        )
        for q in range(parts_ref.shape[0]):
            for kind in range(2):
                parts_ref[q, kind, m] = parts[kind]


def rank_parts(second, returned, acts, rank, quarters):
    micro, _, columns = returned.shape
    return pl.pallas_call(
        functools.partial(part_kernel, micro),
        out_shape=(
            jax.ShapeDtypeStruct((quarters, 2, micro, rank, BLOCK_ROWS), bf16),
            jax.ShapeDtypeStruct((micro, rank, columns), f32),
        ),
        in_specs=[pl.BlockSpec(memory_space=pltpu.VMEM)] * (2 + micro),
        out_specs=(pl.BlockSpec(memory_space=pltpu.VMEM),) * 2,
        compiler_params=params(),
        name="rank_parts",
    )(second, returned, *acts)


def select_kernel(micro, own_slots, rank, slots_ref, first_ref, out, out_ref, sems):
    holders = out_ref.shape[0]
    group = out_ref.shape[1] // micro - rank
    low = own_slots * rank
    chunk = holders // PARTS
    sent = []
    for i in range(PARTS):
        for d in range(i * chunk, (i + 1) * chunk):
            ups = []
            for m in range(micro):
                slot = jnp.minimum(slots_ref[d * micro + m], holders * own_slots - 1)
                owner, k = lax.div(slot, own_slots), lax.rem(slot, own_slots)
                rows = pl.ds(pl.multiple_of(k * rank, rank), rank)
                out_ref[d, m * rank : (m + 1) * rank, :] = first_ref[owner, rows, :]
                held = first_ref[owner, low : low + own_slots * group, :].astype(f32)
                up = held[:group]
                for j in range(1, own_slots):
                    up = jnp.where(k == j, held[j * group : (j + 1) * group], up)
                ups.append(up)
            out_ref[d, micro * rank :, :] = jnp.concatenate(ups, axis=0).astype(bf16)
        some = pl.ds(i * chunk, chunk)
        sent.append(started(out_ref.at[some], out.at[some], sems.at[i]))
    for copy in sent:
        copy.wait()


def selected(slots, first, micro, own_slots, rank, group):
    holders, _, lanes = first.shape
    out = (holders, micro * (rank + group), lanes)
    return pl.pallas_call(
        functools.partial(select_kernel, micro, own_slots, rank),
        out_shape=jax.ShapeDtypeStruct(out, bf16),
        in_specs=[smem(), pl.BlockSpec(memory_space=pltpu.VMEM)],
        out_specs=pl.BlockSpec(memory_space=pl.ANY),
        scratch_shapes=[pltpu.VMEM(out, bf16), pltpu.SemaphoreType.DMA((PARTS,))],
        compiler_params=params(),
        name="selected_pieces",
    )(slots, first)


def gradient_kernel(micro, count, marks_ref, me_ref, ranks_ref, down_ref, product_ref, out_ref):
    rank = ranks_ref.shape[1]
    pieces = down_ref.shape[0]
    for m in range(micro):
        back = (adapter_scale * ranks_ref[m].astype(f32)).T.astype(bf16)
        down = jnp.concatenate(
            [down_ref[p, m * rank : (m + 1) * rank, :] for p in range(pieces)], axis=1
        )
        lora = jnp.dot(back, down, preferred_element_type=f32).astype(bf16).astype(f32)
        part = product_ref[m * BLOCK_ROWS : (m + 1) * BLOCK_ROWS] + lora
        live = marks_ref[me_ref[0] * micro + m] < count
        out_ref[m] = jnp.where(live, part, 0.0).astype(bf16)


def input_gradients(marks, me, count, ranks, second, product):
    micro, rank = ranks.shape[:2]
    rows, width = product.shape
    pieces, _, piece = second.shape
    steps = 2
    return pl.pallas_call(
        functools.partial(gradient_kernel, micro, count),
        grid=(steps,),
        out_shape=jax.ShapeDtypeStruct((micro, BLOCK_ROWS, width), bf16),
        in_specs=[
            smem(),
            smem(),
            pl.BlockSpec(ranks.shape, lambda i: (0, 0, 0)),
            pl.BlockSpec((pieces // steps, micro * rank, piece), lambda i: (i, 0, 0)),
            pl.BlockSpec((rows, width // steps), lambda i: (0, i)),
        ],
        out_specs=pl.BlockSpec((micro, BLOCK_ROWS, width // steps), lambda i: (0, 0, i)),
        compiler_params=pltpu.CompilerParams(vmem_limit_bytes=WIDE_LIMIT),
        cost_estimate=pl.CostEstimate(
            flops=2 * rows * width * rank, bytes_accessed=6 * rows * width, transcendentals=0
        ),
        name="input_gradients",
    )(marks, me, ranks, second, product)


def layer_kernel(micro, count, marks_ref, me_ref, ranks_ref, up_ref, *refs):
    out_ref = refs[-1]
    for m in range(micro):
        total = adapter_scale * tn_dot(ranks_ref[m], up_ref[m].astype(bf16))
        for part_ref in refs[:-1]:
            total += part_ref[m * BLOCK_ROWS : (m + 1) * BLOCK_ROWS, :].astype(f32)
        live = marks_ref[me_ref[0] * micro + m] < count
        out_ref[m] = jnp.where(live, total, 0.0).astype(bf16)


def layer_outputs(marks, me, count, ranks, up, parts):
    micro, _, columns = up.shape
    return pl.pallas_call(
        functools.partial(layer_kernel, micro, count),
        out_shape=jax.ShapeDtypeStruct((micro, BLOCK_ROWS, columns), bf16),
        in_specs=[smem(), smem()] + [pl.BlockSpec(memory_space=pltpu.VMEM)] * (2 + len(parts)),
        out_specs=pl.BlockSpec(memory_space=pltpu.VMEM),
        compiler_params=params(),
        name="layer_outputs",
    )(marks, me, ranks, up, *parts)


def rank_kernel(parts_ref, incoming_ref, ranks_ref, pieces_ref):
    micro, rank = parts_ref.shape[2:4]
    total = parts_ref[0].astype(f32)
    for q in range(1, parts_ref.shape[0]):
        total += parts_ref[q].astype(f32)
    ranks_ref[...] = total.astype(bf16)
    half = rank // 2
    for m in range(micro):
        grad = jnp.dot(ranks_ref[0, m], incoming_ref[m], preferred_element_type=f32)
        grad = (grad * (adapter_scale / BLOCK_ROWS)).astype(bf16)
        for p in range(pieces_ref.shape[0]):
            top = (p % 2) * half
            pieces_ref[p, m] = grad[top : top + half]


def ranks_and_pieces(parts, incoming, holders):
    micro, rank = parts.shape[2:4]
    columns = incoming.shape[2]
    return pl.pallas_call(
        rank_kernel,
        out_shape=(
            jax.ShapeDtypeStruct(parts.shape[1:], bf16),
            jax.ShapeDtypeStruct((holders, micro, rank // 2, columns), bf16),
        ),
        in_specs=[pl.BlockSpec(memory_space=pltpu.VMEM)] * 2,
        out_specs=(pl.BlockSpec(memory_space=pltpu.VMEM),) * 2,
        compiler_params=params(),
        name="ranks_and_pieces",
    )(parts, incoming)


def slot_kernel(marks_ref, first_ref, pieces_ref, out_ref):
    holders, micro = pieces_ref.shape[:2]
    out_ref[...] = jnp.zeros_like(out_ref)
    for d in range(holders):
        marks = [marks_ref[d * micro + m] for m in range(micro)]
        for i in range(out_ref.shape[0]):
            hits = [mark == first_ref[0] + i for mark in marks]

            @pl.when(functools.reduce(jnp.logical_or, hits))
            def _():
                partial = None
                for m in range(micro):
                    term = jnp.where(hits[m], pieces_ref[d, m].astype(f32), 0.0)
                    partial = term if partial is None else partial + term
                out_ref[i, 0] += partial
                out_ref[i, 1] += partial * partial


def slot_sums(marks, first_slot, pieces, own_slots):
    return pl.pallas_call(
        slot_kernel,
        out_shape=jax.ShapeDtypeStruct((own_slots, 2) + pieces.shape[2:], f32),
        in_specs=[smem(), smem(), pl.BlockSpec(memory_space=pltpu.VMEM)],
        out_specs=pl.BlockSpec(memory_space=pltpu.VMEM),
        compiler_params=params(),
        name="slot_sums",
    )(marks, first_slot, pieces)


def place_kernel(core_ref, own_ref, other_ref, sum_ref, square_ref):
    half = own_ref.shape[2]
    low = core_ref[0] == 0
    for k in range(own_ref.shape[0]):
        for kind, out_ref in enumerate((sum_ref, square_ref)):
            own, other = own_ref[k, kind], other_ref[k, kind]
            out_ref[k, :half] = jnp.where(low, own, other)
            out_ref[k, half:] = jnp.where(low, other, own)


def placed(core, own, other):
    own_slots, _, half, columns = own.shape
    shape = jax.ShapeDtypeStruct((own_slots, 2 * half, columns), f32)
    return pl.pallas_call(
        place_kernel,
        out_shape=(shape, shape),
        in_specs=[smem()] + [pl.BlockSpec(memory_space=pltpu.VMEM)] * 2,
        out_specs=(pl.BlockSpec(memory_space=pltpu.VMEM),) * 2,
        compiler_params=params(),
        name="placed_sums",
    )(core, own, other)


def shards(
    activations, cotangent, base_weight, adapter_down, adapter_up, slot_language, block_language
):
    holders = lax.axis_size("dp")
    quarters = lax.axis_size("mp")
    own_slots, width, rank = adapter_down.shape[1:]
    columns = adapter_up.shape[3]
    micro = activations.shape[1]
    rows = micro * BLOCK_ROWS
    piece = width // holders
    up_groups = holders // (columns // LANES)
    up_rows = rank // up_groups
    me = lax.axis_index("dp")

    returned = passed_along(cotangent, "section", -1)[0]
    arrived = [passed_along(activations[:, m : m + 1], "section", 1) for m in range(micro)]

    slot_table = slot_language[0]
    langs = block_language[0, :, 0]

    weight = jnp.swapaxes(base_weight[0], 0, 1)
    flat_cots = returned.reshape(rows, columns)
    cots = [flat_cots] + [
        lax.ppermute(flat_cots, "mp", [(i, (i + k) % quarters) for i in range(quarters)])
        for k in range(1, quarters)
    ]

    down = jnp.swapaxes(adapter_down[0], 1, 2)
    first = packed(langs[None, :], slot_language, down, adapter_up[0], holders)
    first, weight = lax.optimization_barrier((first, weight))
    gathered = lax.all_gather(weight, "dp", axis=0)
    first = exchanged(first, "dp")

    marked = own_slots * (rank + up_rows)
    slots = first[:, marked : marked + micro, 0].astype(jnp.int32).reshape(-1)
    second = selected(slots, first, micro, own_slots, rank, up_rows)
    second, arrived[0], cots[1] = lax.optimization_barrier((second, arrived[0], cots[1]))
    second = exchanged(second, "dp")
    second, cots = lax.optimization_barrier((second, cots))

    parts, up = rank_parts(second, returned, arrived, rank, quarters)
    parts = exchanged(parts, "mp")
    quarter = lax.axis_index("mp").astype(jnp.int32).reshape(1)
    base_parts, back = weight_products(quarter, arrived, cots, gathered)
    parts, base_parts = lax.optimization_barrier((parts, base_parts))
    ranks, pieces = ranks_and_pieces(parts, returned, holders)
    rank_in, rank_back = ranks[0], ranks[1]

    pieces = exchanged(pieces, "dp")
    base_parts = [base_parts[0]] + [
        lax.ppermute(base_parts[k], "mp", [(i, (i + k) % quarters) for i in range(quarters)])
        for k in range(1, quarters)
    ]
    place, count = me.astype(jnp.int32).reshape(1), slot_table.shape[0]
    layer_out = layer_outputs(slots, place, count, rank_in, up, base_parts)[None]
    input_gradient = input_gradients(slots, place, count, rank_back, second, back)[None]
    pieces, input_gradient, layer_out = lax.optimization_barrier(
        (pieces, input_gradient, layer_out)
    )
    other = slot_sums(slots, (own_slots * (me ^ 1)).astype(jnp.int32).reshape(1), pieces, own_slots)
    other = lax.ppermute(other, "dp", [(i, i ^ 1) for i in range(holders)])
    own = slot_sums(slots, (own_slots * me).astype(jnp.int32).reshape(1), pieces, own_slots)
    grad_sum, grad_square = placed((me % 2).astype(jnp.int32).reshape(1), own, other)

    return (layer_out, input_gradient, grad_sum[None], grad_square[None])


def solution(mesh):
    in_specs = (
        P("section", None, "dp", "mp"),
        P("section", None, "dp", "mp"),
        P("section", "mp", "dp"),
        P("section", "dp", "mp", None),
        P("section", "dp", None, "mp"),
        P("section", None),
        P("section", None, "dp"),
    )
    out_specs = (
        P("section", None, "dp", "mp"),
        P("section", None, "dp", "mp"),
        P("section", "dp", None, "mp"),
        P("section", "dp", None, "mp"),
    )
    return jax.shard_map(shards, mesh=mesh, in_specs=in_specs, out_specs=out_specs, check_vma=False)
```
